256 devices in a mesh: variant: 8 (over x, core), mesh: 32 (over z, y).
Axes of the slice: x: 4, y: 4, z: 8, core: 2. Of those that a mesh axis runs over, the one named last changes fastest.
Arguments:
- snapshots: float32 [8, 64, 524288], P('variant', None, 'mesh'), may hold values from -12 to 12, as said below
- ref_index: int32 [1], replicated, may hold values from 0 to 7
- weight_codes: int32 [8], replicated, may hold values from 1 to 16
Outputs:
- new_basis: float32 [64, 524288], P(None, 'mesh')
The draws below stay inside these ranges and needn't reach their ends.
Inputs may be any that keep to these rules, and one draw needn't show every extreme that they name: `snapshots`: each variant's snapshot matrix has full rank 64, and the principal angles between any two variants' spans have tangents below 0.8.
All inputs are finite; a program needn't handle non-finite values.
Results may differ from the reference program's by a relative error of at most 0.0001.
Values sent between devices are 32-bit elements; how exact they have to be, the bound alone decides.
A program may use at most 64 MiB of HBM per device.

```python
import math
import jax
import jax.numpy as jnp
from jax import lax

K = 64
NROWS = 524288
V = 8


def draw_snapshots(key, part):
    first = jax.random.fold_in(jax.random.fold_in(key, 11), 0)
    second = jax.random.fold_in(jax.random.fold_in(key, 11), 1)
    fourth = jax.random.fold_in(jax.random.fold_in(key, 11), 3)
    amplitude = 0.45 * jnp.exp(jax.random.uniform(fourth, (V, K, 1), jnp.float32, jnp.log(0.02 / 0.45), 0.0))
    position = jnp.arange(NROWS, dtype=jnp.float32) / jnp.float32(max(NROWS - 1, 1))
    rising = jnp.exp(jnp.log(4.0) * position)
    base = jax.random.normal(first, (K, NROWS), jnp.float32)
    noise = jax.random.normal(second, (V, K, NROWS), jnp.float32)
    rising = rising / jnp.sqrt(jnp.mean(rising * rising))
    noise = noise * rising[None, None, :]
    return jnp.clip(base[None] + amplitude * noise, -12.0, 12.0)


def place_ends(array, stream_key, smallest, largest):
    extent = array.shape
    index_at = [jax.random.randint(jax.random.fold_in(stream_key, axis), (), 0, extent[axis]) for axis in range(len(extent))]
    array = array.at[tuple(index_at)].set(smallest)
    longest = extent.index(max(extent))
    index_at[longest] = (index_at[longest] + 1) % extent[longest]
    return array.at[tuple(index_at)].set(largest)


def setup_inputs(seed: int = 0) -> dict:
    key_of = jax.random.split(jax.random.key(seed), 4)
    snapshots = draw_snapshots(jax.random.fold_in(key_of[3], 71), 0)
    ref_index = jax.random.randint(key_of[1], (1,), 0, V).astype(jnp.int32)
    weight_codes = place_ends(jax.random.randint(key_of[2], (V,), 1, 17), jax.random.fold_in(key_of[2], 1), 1, 16).astype(jnp.int32)
    return dict(snapshots=snapshots, ref_index=ref_index, weight_codes=weight_codes)


highest = lax.Precision.HIGHEST
atan_coeffs = [(-1.0) ** k / (2 * k + 1) for k in range(24)]
cos_coeffs = [(-1.0) ** k / math.factorial(2 * k) for k in range(24)]
sin_coeffs = [(-1.0) ** k / math.factorial(2 * k + 1) for k in range(24)]

def product(left, right):
    return jnp.dot(left.astype(jnp.float32), right.astype(jnp.float32), precision=highest, preferred_element_type=jnp.float32)

def series(matrix, coeffs):
    eye = jnp.eye(matrix.shape[0], dtype=jnp.float32)
    total = coeffs[-1] * eye
    for coeff in reversed(coeffs[:-1]):
        total = coeff * eye + product(matrix, total)
    return total

def orthonormal(snap):
    lower = jnp.linalg.cholesky(product(snap, snap.T))
    return jax.scipy.linalg.solve_triangular(lower, snap, lower=True)

def reference(snapshots, ref_index, weight_codes):
    base_ref = orthonormal(lax.dynamic_index_in_dim(snapshots, ref_index[0].astype(jnp.int32), 0, keepdims=False))
    codes = weight_codes.astype(jnp.float32)
    weights = codes / jnp.sum(codes)
    blended = jnp.zeros(base_ref.shape, jnp.float32)
    for variant in range(V):
        base_own = orthonormal(snapshots[variant])
        minv = jnp.linalg.inv(product(base_ref, base_own.T))
        tangent = product(minv.T, base_own) - base_ref
        factor = series(product(tangent, tangent.T), atan_coeffs)
        blended = blended + weights[variant] * product(factor, tangent)
    energy = product(blended, blended.T)
    mixed = product(series(energy, cos_coeffs), base_ref) + product(series(energy, sin_coeffs), blended)
    return mixed * jnp.float32(math.sqrt(NROWS))
```

```python
import functools
import math

import jax
import jax.numpy as jnp
from jax import lax
from jax.experimental import pallas as pl
from jax.experimental.pallas import tpu as pltpu
from jax.sharding import PartitionSpec as P

MESH = pl.DeviceIdType.MESH
HIGHEST = lax.Precision.HIGHEST
K = 64
V = 8
HALF = K // 2
atan_coeffs = [(-1.0) ** k / (2 * k + 1) for k in range(24)]
cos_coeffs = [(-1.0) ** k / math.factorial(2 * k) for k in range(24)]
sin_coeffs = [(-1.0) ** k / math.factorial(2 * k + 1) for k in range(24)]
NEWTON_STEPS = 5
NEWTON_START = 2.0 / (1.0 + 1.0 / 1.64)


def dot(left, right, contract=((1,), (0,))):
    return lax.dot_general(
        left, right, (contract, ((), ())), precision=HIGHEST, preferred_element_type=jnp.float32
    )


NT = ((1,), (1,))


def identity():
    rows = lax.broadcasted_iota(jnp.int32, (K, K), 0)
    columns = lax.broadcasted_iota(jnp.int32, (K, K), 1)
    return jnp.where(rows == columns, 1.0, 0.0).astype(jnp.float32)


def pack(square):
    return jnp.concatenate([square[:HALF], square[HALF:]], axis=1)


def unpack(packed):
    return jnp.concatenate([packed[:, :K], packed[:, K:]], axis=0)


def powers(matrix):
    second = dot(matrix, matrix)
    third = dot(second, matrix)
    fourth = dot(second, second)
    return [
        identity(), matrix, second, third, fourth,
        dot(fourth, matrix), dot(fourth, second), dot(fourth, third), dot(fourth, fourth),
    ]


def group(power, coeffs):
    total = coeffs[0] * power[0]
    for i in range(1, len(coeffs)):
        total = total + coeffs[i] * power[i]
    return total


def series(power, coeffs):
    high = group(power, coeffs[16:24])
    middle = group(power, coeffs[8:16]) + dot(power[8], high)
    return group(power, coeffs[0:8]) + dot(power[8], middle)


def inverse_factor(gram):
    rows = lax.broadcasted_iota(jnp.int32, (K, 2 * K), 0)
    columns = lax.broadcasted_iota(jnp.int32, (K, 2 * K), 1)
    top = lax.broadcasted_iota(jnp.int32, (1, 2 * K), 1)

    def step(j, both):
        row = jnp.sum(jnp.where(rows == j, both, 0.0), axis=0, keepdims=True)
        column = jnp.sum(jnp.where(columns == j, both, 0.0), axis=1, keepdims=True)
        pivot = jnp.sum(jnp.where(top == j, row, 0.0), axis=1, keepdims=True)
        return both - jnp.where(rows > j, column, 0.0) * (row / pivot)

    both = lax.fori_loop(0, K, step, jnp.concatenate([gram, identity()], axis=1))
    pivots = jnp.sum(jnp.where(rows == columns, both, 0.0), axis=1, keepdims=True)
    return both[:, K:] * (1.0 / jnp.sqrt(pivots))


def kernel(
    sizes, root_ref, codes_ref, snap_ref, out_ref,
    own, stack_a, stack_b, ends, made,
    gram_y, gram_z, factors, cross_out, cross_x, cross_y, cross_z, terms, energy_x, energy_y, energy_z,
    sent, got, local,
):
    size_z, size_y, chunk, cols_a, cols_b, scale = sizes
    me = lax.axis_index("variant")
    place = lax.axis_index("mesh")
    chip, core = me // 2, lax.rem(me, 2)
    z, y = place // size_y, lax.rem(place, size_y)
    count = iter(range(1000))

    def variant(dx, dc):
        return lax.rem(chip + dx, 4) * 2 + lax.rem(core + dc, 2)

    x_order = [(2, 0), (2, 1), (1, 0), (3, 0), (1, 1), (3, 1), (0, 1)]
    to_x = [{"variant": variant(dx, dc)} for dx, dc in x_order]
    to_y = [{"mesh": z * size_y + lax.rem(y + d, size_y)} for d in range(1, size_y)]
    to_z = [{"mesh": lax.rem(z + d, size_z) * size_y + y} for d in range(1, size_z)]

    def send(source, target, device):
        i = next(count)
        copy = pltpu.make_async_remote_copy(
            src_ref=source, dst_ref=target, send_sem=sent.at[i], recv_sem=got.at[i],
            device_id=device, device_id_type=MESH,
        )
        copy.start()
        return copy

    def share(buffer, slot, value, devices):
        buffer[slot] = value
        return [send(buffer.at[slot], buffer.at[slot], device) for device in devices]

    def total(buffer, copies):
        for copy in copies:
            copy.wait()
        result = buffer[0]
        for i in range(1, buffer.shape[0]):
            result = result + buffer[i]
        return result

    own_copy = pltpu.make_async_copy(snap_ref, own, local.at[0])
    own_copy.start()
    mine = pl.multiple_of(me * chunk, chunk)
    keep_a = pltpu.make_async_copy(
        snap_ref.at[:, pl.ds(mine, cols_a)], stack_a.at[me], local.at[1]
    )
    keep_b = pltpu.make_async_copy(
        snap_ref.at[:, pl.ds(pl.multiple_of(mine + cols_a, 128), cols_b)], stack_b.at[me], local.at[2]
    )
    keep_a.start()
    keep_b.start()

    barrier = pltpu.get_barrier_semaphore()
    for device in to_x + to_y + to_z:
        pl.semaphore_signal(barrier, inc=1, device_id=device, device_id_type=MESH)
    pl.semaphore_wait(barrier, len(to_x) + len(to_y) + len(to_z))

    stage_a = []
    for device in to_x:
        first = pl.multiple_of(device["variant"] * chunk, chunk)
        stage_a.append(send(snap_ref.at[:, pl.ds(first, cols_a)], stack_a.at[me], device))

    own_copy.wait()

    def gram_step(i, gram):
        block = own[:, pl.ds(pl.multiple_of(i * chunk, chunk), chunk)]
        return gram + dot(block, block, NT)

    gram = lax.fori_loop(0, V, gram_step, jnp.zeros((K, K), jnp.float32))
    gram = total(gram_y, share(gram_y, y, pack(gram), to_y))
    gram = total(gram_z, share(gram_z, z, gram, to_z))
    factor = inverse_factor(unpack(gram))
    factor_copies = share(factors, me, pack(factor), to_x)

    stage_b = []
    for device in to_x:
        first = pl.multiple_of(device["variant"] * chunk + cols_a, 128)
        stage_b.append(send(snap_ref.at[:, pl.ds(first, cols_b)], stack_b.at[me], device))

    for copy in factor_copies:
        copy.wait()
    root = root_ref[0]
    root_factor = unpack(factors[root])
    keep_a.wait()
    keep_b.wait()
    for copy in stage_a:
        copy.wait()
    root_a = stack_a[root]
    cross = dot(root_a, stack_a[...].reshape(V * K, cols_a), NT)
    ends[me, :K, :cols_a] = root_a
    for copy in stage_b:
        copy.wait()
    root_b = stack_b[root]
    cross = cross + dot(root_b, stack_b[...].reshape(V * K, cols_b), NT)
    ends[me, :K, cols_a:] = root_b
    for v in range(V):
        cross_out[v] = pack(cross[:, v * K : (v + 1) * K])
    cross_x[me] = cross_out[me]
    cross_copies = [
        send(cross_out.at[device["variant"]], cross_x.at[me], device) for device in to_x
    ]

    ahead, behind, beside = variant(1, 0), variant(3, 0), variant(0, 1)

    def gather_start(row):
        upper, lower, both = pl.ds(row, HALF), pl.ds(row + HALF, HALF), pl.ds(row, K)
        copies = []
        for rows, device in [(upper, ahead), (lower, behind), (lower, ahead), (upper, behind), (both, beside)]:
            part = ends.at[me, rows]
            copies.append(send(part, part, {"variant": device}))
        return copies

    def gather_relay(row, copies):
        for first, rows, origin, device in [
            (copies[0], pl.ds(row, HALF), behind, ahead),
            (copies[1], pl.ds(row + HALF, HALF), ahead, behind),
        ]:
            first.wait_recv()
            part = ends.at[origin, rows]
            copies.append(send(part, part, {"variant": device}))

    def gather_beside(row, copies, needs, origin):
        for i in needs:
            copies[i].wait_recv()
        part = ends.at[origin, pl.ds(row, K)]
        copies.append(send(part, part, {"variant": beside}))

    roots = gather_start(0)
    cross = total(cross_x, cross_copies)
    cross = total(cross_y, share(cross_y, y, cross, to_y))
    cross_copies = share(cross_z, z, cross, to_z)
    gather_relay(0, roots)
    cross = unpack(total(cross_z, cross_copies))

    projection = dot(dot(root_factor, cross), factor, NT)
    flipped = projection.T
    eye = identity()
    inverse = NEWTON_START * projection
    for _ in range(NEWTON_STEPS):
        inverse = dot(inverse, 2.0 * eye - dot(flipped, inverse))
    tangent_gram = dot(inverse, inverse, NT) - eye
    codes = [codes_ref[v] for v in range(V)]
    own_code = jnp.full((K, K), codes_ref[me], jnp.int32).astype(jnp.float32)
    weight = own_code / jnp.full((K, K), sum(codes[1:], codes[0]), jnp.int32).astype(jnp.float32)
    bend = weight * series(powers(tangent_gram), atan_coeffs)
    turn = dot(bend, dot(inverse, factor))
    term_copies = share(terms, me, jnp.concatenate([turn, bend], axis=1), to_x)
    gather_beside(0, roots, (2,), behind)
    gather_beside(0, roots, (3,), ahead)
    gather_beside(0, roots, (5, 6), variant(2, 0))
    for copy in term_copies:
        copy.wait()
    bends = terms[0, :, K:]
    for v in range(1, V):
        bends = bends + terms[v, :, K:]
    back = dot(bends, root_factor)
    mixer = jnp.concatenate(
        [terms[v, :, :K] - jnp.where(root == v, back, 0.0) for v in range(V)], axis=1
    )
    blended_a = dot(mixer, stack_a[...].reshape(V * K, cols_a))
    ends[me, K:, :cols_a] = blended_a
    blended_b = dot(mixer, stack_b[...].reshape(V * K, cols_b))
    ends[me, K:, cols_a:] = blended_b
    energy = dot(blended_a, blended_a, NT) + dot(blended_b, blended_b, NT)
    energy_copies = share(energy_x, me, pack(energy), to_x)
    blends = gather_start(K)
    energy = total(energy_x, energy_copies)
    energy_copies = share(energy_y, y, energy, to_y)
    energy = total(energy_y, energy_copies)
    energy_copies = share(energy_z, z, energy, to_z)
    gather_relay(K, blends)
    energy = unpack(total(energy_z, energy_copies))
    power = powers(energy)
    final = scale * jnp.concatenate(
        [dot(series(power, cos_coeffs), root_factor), series(power, sin_coeffs)], axis=1
    )

    stores = []

    def finish(v):
        made[v] = dot(final, ends[v])
        columns = pl.ds(pl.multiple_of(v * chunk, chunk), chunk)
        store = pltpu.make_async_copy(made.at[v], out_ref.at[:, columns], local.at[3 + len(stores)])
        store.start()
        stores.append(store)

    for i in (4, 7, 8, 9):
        roots[i].wait_recv()
    finish(me)
    gather_beside(K, blends, (2,), behind)
    gather_beside(K, blends, (3,), ahead)
    blends[4].wait_recv()
    finish(beside)
    finish(behind)
    finish(ahead)
    gather_beside(K, blends, (5, 6), variant(2, 0))
    finish(variant(2, 0))
    blends[7].wait_recv()
    finish(variant(3, 1))
    blends[8].wait_recv()
    finish(variant(1, 1))
    blends[9].wait_recv()
    finish(variant(2, 1))
    for copy in roots + blends:
        copy.wait_send()
    for store in stores:
        store.wait()


def on_device(size_z, size_y, snapshots, ref_index, weight_codes):
    snap = snapshots[0]
    rows = snap.shape[1]
    chunk = rows // V
    cols_a = max(128, chunk * 11 // 16 // 128 * 128)
    cols_b = chunk - cols_a
    sizes = (size_z, size_y, chunk, cols_a, cols_b, math.sqrt(rows * size_z * size_y))
    small = (HALF, 2 * K)
    f32 = jnp.float32
    vmem = [
        (K, rows), (V, K, cols_a), (V, K, cols_b), (V, 2 * K, chunk), (V, K, chunk),
        (size_y, *small), (size_z, *small), (V, *small),
        (V, *small), (V, *small), (size_y, *small), (size_z, *small),
        (V, K, 2 * K), (V, *small), (size_y, *small), (size_z, *small),
    ]
    return pl.pallas_call(
        functools.partial(kernel, sizes),
        out_shape=jax.ShapeDtypeStruct((K, rows), f32),
        in_specs=[
            pl.BlockSpec(memory_space=pltpu.SMEM),
            pl.BlockSpec(memory_space=pltpu.SMEM),
            pl.BlockSpec(memory_space=pl.ANY),
        ],
        out_specs=pl.BlockSpec(memory_space=pl.ANY),
        scratch_shapes=[pltpu.VMEM(shape, f32) for shape in vmem]
        + [
            pltpu.SemaphoreType.DMA((100,)),
            pltpu.SemaphoreType.DMA((100,)),
            pltpu.SemaphoreType.DMA((11,)),
        ],
        compiler_params=pltpu.CompilerParams(
            collective_id=0, has_side_effects=True, vmem_limit_bytes=40 << 20
        ),
        name="interpolate",
    )(ref_index, weight_codes, snap)


def solution(mesh, size_y=4):
    size_z = mesh.shape["mesh"] // size_y
    placed = (P("variant", None, "mesh"), P(), P())
    return jax.shard_map(
        functools.partial(on_device, size_z, size_y),
        mesh=mesh, in_specs=placed, out_specs=P(None, "mesh"), check_vma=False,
    )
```

```python
import functools
import math

import jax
import jax.numpy as jnp
from jax import lax
from jax.experimental import pallas as pl
from jax.experimental.pallas import tpu as pltpu
from jax.sharding import PartitionSpec as P

MESH = pl.DeviceIdType.MESH
HIGHEST = lax.Precision.HIGHEST
K = 64
V = 8
HALF = K // 2
atan_coeffs = [(-1.0) ** k / (2 * k + 1) for k in range(24)]
cos_coeffs = [(-1.0) ** k / math.factorial(2 * k) for k in range(24)]
sin_coeffs = [(-1.0) ** k / math.factorial(2 * k + 1) for k in range(24)]
MIDDLE = 2.0 / (1.0 + 1.0 / 1.64)


def dot(left, right, contract=((1,), (0,))):
    return lax.dot_general(
        left, right, (contract, ((), ())), precision=HIGHEST, preferred_element_type=jnp.float32
    )


NT = ((1,), (1,))


def identity():
    rows = lax.broadcasted_iota(jnp.int32, (K, K), 0)
    columns = lax.broadcasted_iota(jnp.int32, (K, K), 1)
    return jnp.where(rows == columns, 1.0, 0.0).astype(jnp.float32)


def pack(square):
    return jnp.concatenate([square[:HALF], square[HALF:]], axis=1)


def unpack(packed):
    return jnp.concatenate([packed[:, :K], packed[:, K:]], axis=0)


def powers(matrix):
    second = dot(matrix, matrix)
    third = dot(second, matrix)
    fourth = dot(second, second)
    return [
        identity(), matrix, second, third, fourth,
        dot(fourth, matrix), dot(fourth, second), dot(fourth, third), dot(fourth, fourth),
    ]


def group(power, coeffs):
    total = coeffs[0] * power[0]
    for i in range(1, len(coeffs)):
        total = total + coeffs[i] * power[i]
    return total


def series(power, coeffs):
    high = group(power, coeffs[16:24])
    middle = group(power, coeffs[8:16]) + dot(power[8], high)
    return group(power, coeffs[0:8]) + dot(power[8], middle)


def inverse_factor(gram):
    rows = lax.broadcasted_iota(jnp.int32, (K, 2 * K), 0)
    columns = lax.broadcasted_iota(jnp.int32, (K, 2 * K), 1)
    top = lax.broadcasted_iota(jnp.int32, (1, 2 * K), 1)

    def step(j, both):
        row = jnp.sum(jnp.where(rows == j, both, 0.0), axis=0, keepdims=True)
        column = jnp.sum(jnp.where(columns == j, both, 0.0), axis=1, keepdims=True)
        pivot = jnp.sum(jnp.where(top == j, row, 0.0), axis=1, keepdims=True)
        return both - jnp.where(rows > j, column, 0.0) * (row / pivot)

    both = lax.fori_loop(0, K, step, jnp.concatenate([gram, identity()], axis=1))
    pivots = jnp.sum(jnp.where(rows == columns, both, 0.0), axis=1, keepdims=True)
    return both[:, K:] * (1.0 / jnp.sqrt(pivots))


def kernel(
    sizes, root_ref, codes_ref, snap_ref, out_ref,
    own, stack_a, stack_b, ends, made,
    gram_y, gram_z, factors, cross_out, cross_x, cross_y, cross_z, terms, energy_x, energy_y, energy_z,
    sent, got, local,
):
    size_z, size_y, chunk, cols_a, cols_b, cols_early, scale = sizes
    me = lax.axis_index("variant")
    place = lax.axis_index("mesh")
    chip, core = me // 2, lax.rem(me, 2)
    z, y = place // size_y, lax.rem(place, size_y)
    count = iter(range(1000))

    def variant(dx, dc):
        return lax.rem(chip + dx, 4) * 2 + lax.rem(core + dc, 2)

    x_order = [(2, 0), (2, 1), (1, 0), (3, 0), (1, 1), (3, 1), (0, 1)]
    to_x = [{"variant": variant(dx, dc)} for dx, dc in x_order]
    to_y = [{"mesh": z * size_y + lax.rem(y + d, size_y)} for d in range(1, size_y)]
    to_z = [{"mesh": lax.rem(z + d, size_z) * size_y + y} for d in range(1, size_z)]

    def send(source, target, device):
        i = next(count)
        copy = pltpu.make_async_remote_copy(
            src_ref=source, dst_ref=target, send_sem=sent.at[i], recv_sem=got.at[i],
            device_id=device, device_id_type=MESH,
        )
        copy.start()
        return copy

    def share(buffer, slot, value, devices):
        buffer[slot] = value
        return [send(buffer.at[slot], buffer.at[slot], device) for device in devices]

    def total(buffer, copies):
        for copy in copies:
            copy.wait()
        result = buffer[0]
        for i in range(1, buffer.shape[0]):
            result = result + buffer[i]
        return result

    own_copy = pltpu.make_async_copy(snap_ref, own, local.at[0])
    own_copy.start()
    mine = pl.multiple_of(me * chunk, chunk)
    keep_a = pltpu.make_async_copy(
        snap_ref.at[:, pl.ds(mine, cols_a)], stack_a.at[me], local.at[1]
    )
    keep_b = pltpu.make_async_copy(
        snap_ref.at[:, pl.ds(pl.multiple_of(mine + cols_a, 128), cols_b)], stack_b.at[me], local.at[2]
    )
    keep_a.start()
    keep_b.start()

    barrier = pltpu.get_barrier_semaphore()
    for device in to_x + to_y + to_z:
        pl.semaphore_signal(barrier, inc=1, device_id=device, device_id_type=MESH)
    pl.semaphore_wait(barrier, len(to_x) + len(to_y) + len(to_z))

    stage_a = []
    for device in to_x:
        first = pl.multiple_of(device["variant"] * chunk, chunk)
        stage_a.append(send(snap_ref.at[:, pl.ds(first, cols_a)], stack_a.at[me], device))

    stage_b = []
    for device in to_x:
        first = pl.multiple_of(device["variant"] * chunk + cols_a, 128)
        stage_b.append(send(snap_ref.at[:, pl.ds(first, cols_b)], stack_b.at[me], device))

    own_copy.wait()

    def gram_step(i, gram):
        block = own[:, pl.ds(pl.multiple_of(i * chunk, chunk), chunk)]
        return gram + dot(block, block, NT)

    gram = lax.fori_loop(0, V, gram_step, jnp.zeros((K, K), jnp.float32))
    gram = total(gram_y, share(gram_y, y, pack(gram), to_y))
    gram = total(gram_z, share(gram_z, z, gram, to_z))
    factor = inverse_factor(unpack(gram))
    factor_copies = share(factors, me, pack(factor), to_x)

    ahead, behind, beside, across = variant(1, 0), variant(3, 0), variant(0, 1), variant(2, 0)

    def gather_start(row, columns):
        upper, lower, both = pl.ds(row, HALF), pl.ds(row + HALF, HALF), pl.ds(row, K)
        copies = []
        for rows, device in [(upper, ahead), (lower, behind), (lower, ahead), (upper, behind), (both, beside)]:
            part = ends.at[me, rows, columns]
            copies.append(send(part, part, {"variant": device}))
        return copies

    def gather_relay(row, columns, copies):
        for first, rows, origin, device in [
            (copies[0], pl.ds(row, HALF), behind, ahead),
            (copies[1], pl.ds(row + HALF, HALF), ahead, behind),
        ]:
            first.wait_recv()
            part = ends.at[origin, rows, columns]
            copies.append(send(part, part, {"variant": device}))

    def gather_beside(row, groups, needs, origin):
        for copies in groups:
            for i in needs:
                copies[i].wait_recv()
        part = ends.at[origin, pl.ds(row, K)]
        return send(part, part, {"variant": beside})

    part_a, part_b = pl.ds(0, cols_early), pl.ds(cols_early, chunk - cols_early)

    keep_a.wait()
    keep_b.wait()
    for copy in stage_a:
        copy.wait()
    root = root_ref[0]
    root_a = stack_a[root]
    ends[me, :K, :cols_a] = root_a
    roots_a = gather_start(0, part_a)
    cross = dot(root_a, stack_a[...].reshape(V * K, cols_a), NT)
    for copy in stage_b:
        copy.wait()
    root_b = stack_b[root]
    cross = cross + dot(root_b, stack_b[...].reshape(V * K, cols_b), NT)
    for v in range(V):
        cross_out[v] = pack(cross[:, v * K : (v + 1) * K])
    cross_x[me] = cross_out[me]
    cross_copies = [
        send(cross_out.at[device["variant"]], cross_x.at[me], device) for device in to_x
    ]
    ends[me, :K, cols_a:] = root_b
    roots_b = gather_start(0, part_b)
    cross = total(cross_x, cross_copies)
    cross_copies = share(cross_y, y, cross, to_y)
    gather_relay(0, part_a, roots_a)
    cross = total(cross_y, cross_copies)
    cross_copies = share(cross_z, z, cross, to_z)
    gather_relay(0, part_b, roots_b)
    for copy in factor_copies:
        copy.wait()
    root_factor = unpack(factors[root])
    cross = unpack(total(cross_z, cross_copies))

    projection = dot(dot(root_factor, cross), factor, NT)
    eye = identity()
    rest = eye - MIDDLE * dot(projection, projection, NT)
    rest_2 = dot(rest, rest)
    rest_4 = dot(rest_2, rest_2)
    rest_8 = dot(rest_4, rest_4)
    inverse = eye + rest
    for rest in (rest_2, rest_4, rest_8):
        inverse = inverse + dot(inverse, rest)
    inverse = MIDDLE * inverse
    tangent_gram = inverse - eye
    turn = dot(inverse, dot(projection, factor))
    codes = [codes_ref[v] for v in range(V)]
    own_code = jnp.full((K, K), codes_ref[me], jnp.int32).astype(jnp.float32)
    weight = own_code / jnp.full((K, K), sum(codes[1:], codes[0]), jnp.int32).astype(jnp.float32)
    bend = weight * series(powers(tangent_gram), atan_coeffs)
    turn = dot(bend, turn)
    term_copies = share(terms, me, jnp.concatenate([turn, bend], axis=1), to_x)
    roots = [
        gather_beside(0, (roots_a, roots_b), (2,), behind),
        gather_beside(0, (roots_a, roots_b), (3,), ahead),
        gather_beside(0, (roots_a, roots_b), (5, 6), across),
    ]
    for copy in term_copies:
        copy.wait()
    bends = terms[0, :, K:]
    for v in range(1, V):
        bends = bends + terms[v, :, K:]
    back = dot(bends, root_factor)
    mixer = jnp.concatenate(
        [terms[v, :, :K] - jnp.where(root == v, back, 0.0) for v in range(V)], axis=1
    )
    blended_a = dot(mixer, stack_a[:, :, :cols_early].reshape(V * K, cols_early))
    ends[me, K:, :cols_early] = blended_a
    blends_a = gather_start(K, part_a)
    blended_b = dot(mixer, stack_a[:, :, cols_early:].reshape(V * K, cols_a - cols_early))
    ends[me, K:, cols_early:cols_a] = blended_b
    blended_c = dot(mixer, stack_b[...].reshape(V * K, cols_b))
    ends[me, K:, cols_a:] = blended_c
    energy = dot(blended_a, blended_a, NT)
    energy = energy + dot(blended_b, blended_b, NT) + dot(blended_c, blended_c, NT)
    energy_copies = share(energy_x, me, pack(energy), to_x)
    blends_b = gather_start(K, part_b)
    energy = total(energy_x, energy_copies)
    energy_copies = share(energy_y, y, energy, to_y)
    gather_relay(K, part_a, blends_a)
    energy = total(energy_y, energy_copies)
    energy_copies = share(energy_z, z, energy, to_z)
    gather_relay(K, part_b, blends_b)
    energy = unpack(total(energy_z, energy_copies))
    power = powers(energy)
    final = scale * jnp.concatenate(
        [dot(series(power, cos_coeffs), root_factor), series(power, sin_coeffs)], axis=1
    )

    stores = []

    def finish(v):
        made[v] = dot(final, ends[v])
        columns = pl.ds(pl.multiple_of(v * chunk, chunk), chunk)
        store = pltpu.make_async_copy(made.at[v], out_ref.at[:, columns], local.at[3 + len(stores)])
        store.start()
        stores.append(store)

    groups = (blends_a, blends_b)
    for copy in [roots_a[4], roots_b[4], *roots]:
        copy.wait_recv()
    finish(me)
    blends = [gather_beside(K, groups, (2,), behind), gather_beside(K, groups, (3,), ahead)]
    for copies in groups:
        copies[4].wait_recv()
    finish(beside)
    finish(behind)
    finish(ahead)
    blends.append(gather_beside(K, groups, (5, 6), across))
    finish(across)
    for copy, dx in zip(blends, (3, 1, 2)):
        copy.wait_recv()
        finish(variant(dx, 1))
    for copy in roots_a + roots_b + roots + blends_a + blends_b + blends:
        copy.wait_send()
    for store in stores:
        store.wait()


def on_device(size_z, size_y, snapshots, ref_index, weight_codes):
    snap = snapshots[0]
    rows = snap.shape[1]
    chunk = rows // V
    cols_a = max(128, chunk * 11 // 16 // 128 * 128)
    cols_b = chunk - cols_a
    cols_early = max(128, chunk // 4 // 128 * 128)
    sizes = (size_z, size_y, chunk, cols_a, cols_b, cols_early, math.sqrt(rows * size_z * size_y))
    small = (HALF, 2 * K)
    f32 = jnp.float32
    vmem = [
        (K, rows), (V, K, cols_a), (V, K, cols_b), (V, 2 * K, chunk), (V, K, chunk),
        (size_y, *small), (size_z, *small), (V, *small),
        (V, *small), (V, *small), (size_y, *small), (size_z, *small),
        (V, K, 2 * K), (V, *small), (size_y, *small), (size_z, *small),
    ]
    return pl.pallas_call(
        functools.partial(kernel, sizes),
        out_shape=jax.ShapeDtypeStruct((K, rows), f32),
        in_specs=[
            pl.BlockSpec(memory_space=pltpu.SMEM),
            pl.BlockSpec(memory_space=pltpu.SMEM),
            pl.BlockSpec(memory_space=pltpu.HBM),
        ],
        out_specs=pl.BlockSpec(memory_space=pl.ANY),
        scratch_shapes=[pltpu.VMEM(shape, f32) for shape in vmem]
        + [
            pltpu.SemaphoreType.DMA((120,)),
            pltpu.SemaphoreType.DMA((120,)),
            pltpu.SemaphoreType.DMA((11,)),
        ],
        compiler_params=pltpu.CompilerParams(
            collective_id=0, has_side_effects=True, vmem_limit_bytes=40 << 20
        ),
        name="interpolate",
    )(ref_index, weight_codes, pltpu.with_memory_space_constraint(snap, pltpu.HBM))


def solution(mesh, size_y=4):
    size_z = mesh.shape["mesh"] // size_y
    placed = (P("variant", None, "mesh"), P(), P())
    return jax.shard_map(
        functools.partial(on_device, size_z, size_y),
        mesh=mesh, in_specs=placed, out_specs=P(None, "mesh"), check_vma=False,
    )
```

```python
import functools
import math

import jax
import jax.numpy as jnp
from jax import lax
from jax.experimental import pallas as pl
from jax.experimental.pallas import tpu as pltpu
from jax.sharding import PartitionSpec as P

MESH = pl.DeviceIdType.MESH
HIGHEST = lax.Precision.HIGHEST
K = 64
V = 8
HALF = K // 2
atan_coeffs = [(-1.0) ** k / (2 * k + 1) for k in range(24)]
cos_coeffs = [(-1.0) ** k / math.factorial(2 * k) for k in range(24)]
sin_coeffs = [(-1.0) ** k / math.factorial(2 * k + 1) for k in range(24)]
MIDDLE = 2.0 / (1.0 + 1.0 / 1.64)


def dot(left, right, contract=((1,), (0,))):
    return lax.dot_general(
        left, right, (contract, ((), ())), precision=HIGHEST, preferred_element_type=jnp.float32
    )


NT = ((1,), (1,))
NN = ((1,), (0,))


def split(array):
    high = array.astype(jnp.bfloat16)
    return high, (array - high.astype(jnp.float32)).astype(jnp.bfloat16)


def split_dot(left, high, low, contract):
    rows = left.shape[0]
    left_high, left_low = split(left)
    both = lax.dot_general(
        jnp.concatenate([left_high, left_low], axis=0), high, (contract, ((), ())),
        preferred_element_type=jnp.float32,
    )
    other = lax.dot_general(
        left_high, low, (contract, ((), ())), preferred_element_type=jnp.float32
    )
    return both[:rows] + (both[rows:] + other)


def identity():
    rows = lax.broadcasted_iota(jnp.int32, (K, K), 0)
    columns = lax.broadcasted_iota(jnp.int32, (K, K), 1)
    return jnp.where(rows == columns, 1.0, 0.0).astype(jnp.float32)


def pack(square):
    return jnp.concatenate([square[:HALF], square[HALF:]], axis=1)


def unpack(packed):
    return jnp.concatenate([packed[:, :K], packed[:, K:]], axis=0)


def powers(matrix):
    second = dot(matrix, matrix)
    third = dot(second, matrix)
    fourth = dot(second, second)
    return [
        identity(), matrix, second, third, fourth,
        dot(fourth, matrix), dot(fourth, second), dot(fourth, third), dot(fourth, fourth),
    ]


def group(power, coeffs):
    total = coeffs[0] * power[0]
    for i in range(1, len(coeffs)):
        total = total + coeffs[i] * power[i]
    return total


def series(power, coeffs):
    high = group(power, coeffs[16:24])
    middle = group(power, coeffs[8:16]) + dot(power[8], high)
    return group(power, coeffs[0:8]) + dot(power[8], middle)


def inverse_factor(gram):
    rows = lax.broadcasted_iota(jnp.int32, (K, 2 * K), 0)
    columns = lax.broadcasted_iota(jnp.int32, (K, 2 * K), 1)
    top = lax.broadcasted_iota(jnp.int32, (1, 2 * K), 1)

    def step(j, both):
        row = jnp.sum(jnp.where(rows == j, both, 0.0), axis=0, keepdims=True)
        column = jnp.sum(jnp.where(columns == j, both, 0.0), axis=1, keepdims=True)
        pivot = jnp.sum(jnp.where(top == j, row, 0.0), axis=1, keepdims=True)
        return both - jnp.where(rows > j, column, 0.0) * (row / pivot)

    both = lax.fori_loop(0, K, step, jnp.concatenate([gram, identity()], axis=1))
    pivots = jnp.sum(jnp.where(rows == columns, both, 0.0), axis=1, keepdims=True)
    return both[:, K:] * (1.0 / jnp.sqrt(pivots))


def kernel(
    sizes, root_ref, codes_ref, snap_ref, out_ref,
    own, stack_a, stack_b, ends, made,
    gram_y, gram_z, factors, cross_out, cross_x, cross_y, cross_z, terms, energy_x, energy_y, energy_z,
    high_a, low_a, high_b, low_b, sent, got, local,
):
    size_z, size_y, chunk, cols_a, cols_b, cols_early, scale = sizes
    me = lax.axis_index("variant")
    place = lax.axis_index("mesh")
    chip, core = me // 2, lax.rem(me, 2)
    z, y = place // size_y, lax.rem(place, size_y)
    count = iter(range(1000))

    def variant(dx, dc):
        return lax.rem(chip + dx, 4) * 2 + lax.rem(core + dc, 2)

    x_order = [(2, 0), (2, 1), (1, 0), (3, 0), (1, 1), (3, 1), (0, 1)]
    to_x = [{"variant": variant(dx, dc)} for dx, dc in x_order]
    to_y = [{"mesh": z * size_y + lax.rem(y + d, size_y)} for d in range(1, size_y)]
    to_z = [{"mesh": lax.rem(z + d, size_z) * size_y + y} for d in range(1, size_z)]

    def send(source, target, device):
        i = next(count)
        copy = pltpu.make_async_remote_copy(
            src_ref=source, dst_ref=target, send_sem=sent.at[i], recv_sem=got.at[i],
            device_id=device, device_id_type=MESH,
        )
        copy.start()
        return copy

    def share(buffer, slot, value, devices):
        buffer[slot] = value
        return [send(buffer.at[slot], buffer.at[slot], device) for device in devices]

    def total(buffer, copies):
        for copy in copies:
            copy.wait()
        result = buffer[0]
        for i in range(1, buffer.shape[0]):
            result = result + buffer[i]
        return result

    own_copy = pltpu.make_async_copy(snap_ref, own, local.at[0])
    own_copy.start()
    mine = pl.multiple_of(me * chunk, chunk)
    keep_a = pltpu.make_async_copy(
        snap_ref.at[:, pl.ds(mine, cols_a)], stack_a.at[me], local.at[1]
    )
    keep_b = pltpu.make_async_copy(
        snap_ref.at[:, pl.ds(pl.multiple_of(mine + cols_a, 128), cols_b)], stack_b.at[me], local.at[2]
    )
    keep_a.start()
    keep_b.start()

    barrier = pltpu.get_barrier_semaphore()
    for device in to_x + to_y + to_z:
        pl.semaphore_signal(barrier, inc=1, device_id=device, device_id_type=MESH)
    pl.semaphore_wait(barrier, len(to_x) + len(to_y) + len(to_z))

    stage_a = []
    for device in to_x:
        first = pl.multiple_of(device["variant"] * chunk, chunk)
        stage_a.append(send(snap_ref.at[:, pl.ds(first, cols_a)], stack_a.at[me], device))

    stage_b = []
    for device in to_x:
        first = pl.multiple_of(device["variant"] * chunk + cols_a, 128)
        stage_b.append(send(snap_ref.at[:, pl.ds(first, cols_b)], stack_b.at[me], device))

    own_copy.wait()

    def gram_step(i, gram):
        block = own[:, pl.ds(pl.multiple_of(i * chunk, chunk), chunk)]
        return gram + dot(block, block, NT)

    gram = lax.fori_loop(0, V, gram_step, jnp.zeros((K, K), jnp.float32))
    gram = total(gram_y, share(gram_y, y, pack(gram), to_y))
    gram = total(gram_z, share(gram_z, z, gram, to_z))
    factor = inverse_factor(unpack(gram))
    factor_copies = share(factors, me, pack(factor), to_x)

    ahead, behind, beside, across = variant(1, 0), variant(3, 0), variant(0, 1), variant(2, 0)

    def gather_start(row, columns):
        upper, lower, both = pl.ds(row, HALF), pl.ds(row + HALF, HALF), pl.ds(row, K)
        copies = []
        for rows, device in [(upper, ahead), (lower, behind), (lower, ahead), (upper, behind), (both, beside)]:
            part = ends.at[me, rows, columns]
            copies.append(send(part, part, {"variant": device}))
        return copies

    def gather_relay(row, columns, copies):
        for first, rows, origin, device in [
            (copies[0], pl.ds(row, HALF), behind, ahead),
            (copies[1], pl.ds(row + HALF, HALF), ahead, behind),
        ]:
            first.wait_recv()
            part = ends.at[origin, rows, columns]
            copies.append(send(part, part, {"variant": device}))

    def gather_beside(row, groups, needs, origin):
        for copies in groups:
            for i in needs:
                copies[i].wait_recv()
        part = ends.at[origin, pl.ds(row, K)]
        return send(part, part, {"variant": beside})

    part_a, part_b = pl.ds(0, cols_early), pl.ds(cols_early, chunk - cols_early)

    keep_a.wait()
    keep_b.wait()
    for copy in stage_a:
        copy.wait()
    root = root_ref[0]
    root_a = stack_a[root]
    ends[me, :K, :cols_a] = root_a
    roots_a = gather_start(0, part_a)
    high_a[...], low_a[...] = split(stack_a[...].reshape(V * K, cols_a))
    cross = split_dot(root_a, high_a[...], low_a[...], NT)
    for copy in stage_b:
        copy.wait()
    root_b = stack_b[root]
    high_b[...], low_b[...] = split(stack_b[...].reshape(V * K, cols_b))
    cross = cross + split_dot(root_b, high_b[...], low_b[...], NT)
    for v in range(V):
        cross_out[v] = pack(cross[:, v * K : (v + 1) * K])
    cross_x[me] = cross_out[me]
    cross_copies = [
        send(cross_out.at[device["variant"]], cross_x.at[me], device) for device in to_x
    ]
    ends[me, :K, cols_a:] = root_b
    roots_b = gather_start(0, part_b)
    cross = total(cross_x, cross_copies)
    cross_copies = share(cross_y, y, cross, to_y)
    gather_relay(0, part_a, roots_a)
    cross = total(cross_y, cross_copies)
    cross_copies = share(cross_z, z, cross, to_z)
    gather_relay(0, part_b, roots_b)
    for copy in factor_copies:
        copy.wait()
    root_factor = unpack(factors[root])
    cross = unpack(total(cross_z, cross_copies))

    projection = dot(dot(root_factor, cross), factor, NT)
    eye = identity()
    rest = eye - MIDDLE * dot(projection, projection, NT)
    rest_2 = dot(rest, rest)
    rest_4 = dot(rest_2, rest_2)
    rest_8 = dot(rest_4, rest_4)
    inverse = eye + rest
    for rest in (rest_2, rest_4, rest_8):
        inverse = inverse + dot(inverse, rest)
    inverse = MIDDLE * inverse
    tangent_gram = inverse - eye
    turn = dot(inverse, dot(projection, factor))
    codes = [codes_ref[v] for v in range(V)]
    own_code = jnp.full((K, K), codes_ref[me], jnp.int32).astype(jnp.float32)
    weight = own_code / jnp.full((K, K), sum(codes[1:], codes[0]), jnp.int32).astype(jnp.float32)
    bend = weight * series(powers(tangent_gram), atan_coeffs)
    turn = dot(bend, turn)
    term_copies = share(terms, me, jnp.concatenate([turn, bend], axis=1), to_x)
    roots = [
        gather_beside(0, (roots_a, roots_b), (2,), behind),
        gather_beside(0, (roots_a, roots_b), (3,), ahead),
        gather_beside(0, (roots_a, roots_b), (5, 6), across),
    ]
    for copy in term_copies:
        copy.wait()
    bends = terms[0, :, K:]
    for v in range(1, V):
        bends = bends + terms[v, :, K:]
    back = dot(bends, root_factor)
    mixer = jnp.concatenate(
        [terms[v, :, :K] - jnp.where(root == v, back, 0.0) for v in range(V)], axis=1
    )
    blended_a = split_dot(mixer, high_a[:, :cols_early], low_a[:, :cols_early], NN)
    ends[me, K:, :cols_early] = blended_a
    blends_a = gather_start(K, part_a)
    blended_b = split_dot(mixer, high_a[:, cols_early:], low_a[:, cols_early:], NN)
    ends[me, K:, cols_early:cols_a] = blended_b
    blended_c = split_dot(mixer, high_b[...], low_b[...], NN)
    ends[me, K:, cols_a:] = blended_c
    energy = jnp.zeros((K, K), jnp.float32)
    for blended in (blended_a, blended_b, blended_c):
        energy = energy + split_dot(blended, *split(blended), NT)
    energy_copies = share(energy_x, me, pack(energy), to_x)
    blends_b = gather_start(K, part_b)
    energy = total(energy_x, energy_copies)
    energy_copies = share(energy_y, y, energy, to_y)
    gather_relay(K, part_a, blends_a)
    energy = total(energy_y, energy_copies)
    energy_copies = share(energy_z, z, energy, to_z)
    gather_relay(K, part_b, blends_b)
    energy = unpack(total(energy_z, energy_copies))
    groups = (blends_a, blends_b)
    blends = [gather_beside(K, groups, (2,), behind), gather_beside(K, groups, (3,), ahead)]
    power = powers(energy)
    final = scale * jnp.concatenate(
        [dot(series(power, cos_coeffs), root_factor), series(power, sin_coeffs)], axis=1
    )

    stores = []

    def finish(v):
        made[v] = split_dot(final, *split(ends[v]), NN)
        columns = pl.ds(pl.multiple_of(v * chunk, chunk), chunk)
        store = pltpu.make_async_copy(made.at[v], out_ref.at[:, columns], local.at[3 + len(stores)])
        store.start()
        stores.append(store)

    for copy in [roots_a[4], roots_b[4], *roots]:
        copy.wait_recv()
    finish(me)
    finish(behind)
    finish(ahead)
    for copies in groups:
        copies[4].wait_recv()
    finish(beside)
    for copy, dx in zip(blends, (3, 1)):
        copy.wait_recv()
        finish(variant(dx, 1))
    blends.append(gather_beside(K, groups, (5, 6), across))
    finish(across)
    blends[2].wait_recv()
    finish(variant(2, 1))
    for copy in roots_a + roots_b + roots + blends_a + blends_b + blends:
        copy.wait_send()
    for store in stores:
        store.wait()


def on_device(size_z, size_y, snapshots, ref_index, weight_codes):
    snap = snapshots[0]
    rows = snap.shape[1]
    chunk = rows // V
    cols_a = max(256, chunk * 13 // 16 // 128 * 128)
    cols_b = chunk - cols_a
    cols_early = max(128, chunk // 8 // 128 * 128)
    sizes = (size_z, size_y, chunk, cols_a, cols_b, cols_early, math.sqrt(rows * size_z * size_y))
    small = (HALF, 2 * K)
    f32 = jnp.float32
    vmem = [
        (K, rows), (V, K, cols_a), (V, K, cols_b), (V, 2 * K, chunk), (V, K, chunk),
        (size_y, *small), (size_z, *small), (V, *small),
        (V, *small), (V, *small), (size_y, *small), (size_z, *small),
        (V, K, 2 * K), (V, *small), (size_y, *small), (size_z, *small),
    ]
    return pl.pallas_call(
        functools.partial(kernel, sizes),
        out_shape=jax.ShapeDtypeStruct((K, rows), f32),
        in_specs=[
            pl.BlockSpec(memory_space=pltpu.SMEM),
            pl.BlockSpec(memory_space=pltpu.SMEM),
            pl.BlockSpec(memory_space=pltpu.HBM),
        ],
        out_specs=pl.BlockSpec(memory_space=pl.ANY),
        scratch_shapes=[pltpu.VMEM(shape, f32) for shape in vmem]
        + [pltpu.VMEM((V * K, cols), jnp.bfloat16) for cols in (cols_a, cols_a, cols_b, cols_b)]
        + [
            pltpu.SemaphoreType.DMA((120,)),
            pltpu.SemaphoreType.DMA((120,)),
            pltpu.SemaphoreType.DMA((11,)),
        ],
        compiler_params=pltpu.CompilerParams(
            collective_id=0, has_side_effects=True, vmem_limit_bytes=40 << 20
        ),
        name="interpolate",
    )(ref_index, weight_codes, pltpu.with_memory_space_constraint(snap, pltpu.HBM))


def solution(mesh, size_y=4):
    size_z = mesh.shape["mesh"] // size_y
    placed = (P("variant", None, "mesh"), P(), P())
    return jax.shard_map(
        functools.partial(on_device, size_z, size_y),
        mesh=mesh, in_specs=placed, out_specs=P(None, "mesh"), check_vma=False,
    )
```

```python
import functools
import math

import jax
import jax.numpy as jnp
from jax import lax
from jax.experimental import pallas as pl
from jax.experimental.pallas import tpu as pltpu
from jax.sharding import PartitionSpec as P

MESH = pl.DeviceIdType.MESH
HIGHEST = lax.Precision.HIGHEST
K = 64
V = 8
HALF = K // 2
atan_coeffs = [(-1.0) ** k / (2 * k + 1) for k in range(24)]
cos_coeffs = [(-1.0) ** k / math.factorial(2 * k) for k in range(24)]
sin_coeffs = [(-1.0) ** k / math.factorial(2 * k + 1) for k in range(24)]
MIDDLE = 2.0 / (1.0 + 1.0 / 1.64)


def dot(left, right, contract=((1,), (0,))):
    return lax.dot_general(
        left, right, (contract, ((), ())), precision=HIGHEST, preferred_element_type=jnp.float32
    )


NT = ((1,), (1,))
NN = ((1,), (0,))


def split(array):
    high = array.astype(jnp.bfloat16)
    return high, (array - high.astype(jnp.float32)).astype(jnp.bfloat16)


def split_dot(left, high, low, contract):
    rows = left.shape[0]
    left_high, left_low = split(left)
    both = lax.dot_general(
        jnp.concatenate([left_high, left_low], axis=0), high, (contract, ((), ())),
        preferred_element_type=jnp.float32,
    )
    other = lax.dot_general(
        left_high, low, (contract, ((), ())), preferred_element_type=jnp.float32
    )
    return both[:rows] + (both[rows:] + other)


def identity():
    rows = lax.broadcasted_iota(jnp.int32, (K, K), 0)
    columns = lax.broadcasted_iota(jnp.int32, (K, K), 1)
    return jnp.where(rows == columns, 1.0, 0.0).astype(jnp.float32)


def pack(square):
    return jnp.concatenate([square[:HALF], square[HALF:]], axis=1)


def unpack(packed):
    return jnp.concatenate([packed[:, :K], packed[:, K:]], axis=0)


def powers(matrix):
    second = dot(matrix, matrix)
    third = dot(second, matrix)
    fourth = dot(second, second)
    return [
        identity(), matrix, second, third, fourth,
        dot(fourth, matrix), dot(fourth, second), dot(fourth, third), dot(fourth, fourth),
    ]


def group(power, coeffs):
    total = coeffs[0] * power[0]
    for i in range(1, len(coeffs)):
        total = total + coeffs[i] * power[i]
    return total


def series(power, coeffs):
    high = group(power, coeffs[16:24])
    middle = group(power, coeffs[8:16]) + dot(power[8], high)
    return group(power, coeffs[0:8]) + dot(power[8], middle)


def inverse_factor(gram):
    rows = lax.broadcasted_iota(jnp.int32, (K, 2 * K), 0)
    columns = lax.broadcasted_iota(jnp.int32, (K, 2 * K), 1)
    top = lax.broadcasted_iota(jnp.int32, (1, 2 * K), 1)

    def step(j, both):
        row = jnp.sum(jnp.where(rows == j, both, 0.0), axis=0, keepdims=True)
        column = jnp.sum(jnp.where(columns == j, both, 0.0), axis=1, keepdims=True)
        pivot = jnp.sum(jnp.where(top == j, row, 0.0), axis=1, keepdims=True)
        return both - jnp.where(rows > j, column, 0.0) * (row / pivot)

    both = lax.fori_loop(0, K, step, jnp.concatenate([gram, identity()], axis=1))
    pivots = jnp.sum(jnp.where(rows == columns, both, 0.0), axis=1, keepdims=True)
    return both[:, K:] * (1.0 / jnp.sqrt(pivots))


def kernel(
    sizes, root_ref, codes_ref, snap_ref, out_ref,
    own, stack_a, stack_b, ends, made,
    gram_y, gram_z, factors, cross_out, cross_x, cross_y, cross_z, terms, energy_x, energy_y, energy_z,
    high_a, low_a, high_b, low_b, sent, got, local,
):
    size_z, size_y, chunk, cols_a, cols_b, cols_early, scale = sizes
    me = lax.axis_index("variant")
    place = lax.axis_index("mesh")
    chip, core = me // 2, lax.rem(me, 2)
    z, y = place // size_y, lax.rem(place, size_y)
    count = iter(range(1000))

    def variant(dx, dc):
        return lax.rem(chip + dx, 4) * 2 + lax.rem(core + dc, 2)

    x_order = [(2, 0), (2, 1), (1, 0), (3, 0), (1, 1), (3, 1), (0, 1)]
    to_x = [{"variant": variant(dx, dc)} for dx, dc in x_order]
    to_y = [{"mesh": z * size_y + lax.rem(y + d, size_y)} for d in range(1, size_y)]
    to_z = [{"mesh": lax.rem(z + d, size_z) * size_y + y} for d in range(1, size_z)]

    def send(source, target, device):
        i = next(count)
        copy = pltpu.make_async_remote_copy(
            src_ref=source, dst_ref=target, send_sem=sent.at[i], recv_sem=got.at[i],
            device_id=device, device_id_type=MESH,
        )
        copy.start()
        return copy

    def share(buffer, slot, value, devices):
        buffer[slot] = value
        return [send(buffer.at[slot], buffer.at[slot], device) for device in devices]

    def total(buffer, copies):
        for copy in copies:
            copy.wait()
        result = buffer[0]
        for i in range(1, buffer.shape[0]):
            result = result + buffer[i]
        return result

    own_copy = pltpu.make_async_copy(snap_ref, own, local.at[0])
    own_copy.start()
    mine = pl.multiple_of(me * chunk, chunk)
    keep_a = pltpu.make_async_copy(
        snap_ref.at[:, pl.ds(mine, cols_a)], stack_a.at[me], local.at[1]
    )
    keep_b = pltpu.make_async_copy(
        snap_ref.at[:, pl.ds(pl.multiple_of(mine + cols_a, 128), cols_b)], stack_b.at[me], local.at[2]
    )
    keep_a.start()
    keep_b.start()

    barrier = pltpu.get_barrier_semaphore()
    for device in to_x + to_y + to_z:
        pl.semaphore_signal(barrier, inc=1, device_id=device, device_id_type=MESH)
    pl.semaphore_wait(barrier, len(to_x) + len(to_y) + len(to_z))

    stage_a = []
    for device in to_x:
        first = pl.multiple_of(device["variant"] * chunk, chunk)
        stage_a.append(send(snap_ref.at[:, pl.ds(first, cols_a)], stack_a.at[me], device))

    stage_b = []
    for device in to_x:
        first = pl.multiple_of(device["variant"] * chunk + cols_a, 128)
        stage_b.append(send(snap_ref.at[:, pl.ds(first, cols_b)], stack_b.at[me], device))

    own_copy.wait()

    def gram_step(i, gram):
        block = own[:, pl.ds(pl.multiple_of(i * chunk, chunk), chunk)]
        return gram + dot(block, block, NT)

    gram = lax.fori_loop(0, V, gram_step, jnp.zeros((K, K), jnp.float32))
    gram = total(gram_y, share(gram_y, y, pack(gram), to_y))
    gram = total(gram_z, share(gram_z, z, gram, to_z))
    factor = inverse_factor(unpack(gram))
    ahead, behind, beside, across = variant(1, 0), variant(3, 0), variant(0, 1), variant(2, 0)
    factor_copies = share(
        factors, me, pack(factor), [{"variant": v} for v in (across, ahead, behind, beside)]
    )

    def gather_start(row, columns):
        upper, lower, both = pl.ds(row, HALF), pl.ds(row + HALF, HALF), pl.ds(row, K)
        copies = []
        for rows, device in [(upper, ahead), (lower, behind), (lower, ahead), (upper, behind), (both, beside)]:
            part = ends.at[me, rows, columns]
            copies.append(send(part, part, {"variant": device}))
        return copies

    def gather_relay(row, columns, copies):
        for first, rows, origin, device in [
            (copies[0], pl.ds(row, HALF), behind, ahead),
            (copies[1], pl.ds(row + HALF, HALF), ahead, behind),
        ]:
            first.wait_recv()
            part = ends.at[origin, rows, columns]
            copies.append(send(part, part, {"variant": device}))

    def gather_beside(row, groups, needs, origin, columns):
        for copies in groups:
            for i in needs:
                copies[i].wait_recv()
        part = ends.at[origin, pl.ds(row, K), columns]
        return send(part, part, {"variant": beside})

    whole = pl.ds(0, chunk)
    part_a, part_b = pl.ds(0, chunk // 4), pl.ds(chunk // 4, chunk // 2)
    root_last = pl.ds(chunk - chunk // 4, chunk // 4)

    keep_a.wait()
    keep_b.wait()
    for copy in stage_a:
        copy.wait()
    root = root_ref[0]
    root_a = stack_a[root]
    ends[me, :K, :cols_a] = root_a
    roots_a = gather_start(0, part_a)
    high_a[...], low_a[...] = split(stack_a[...].reshape(V * K, cols_a))
    cross = split_dot(root_a, high_a[...], low_a[...], NT)
    for copy in stage_b:
        copy.wait()
    root_b = stack_b[root]
    high_b[...], low_b[...] = split(stack_b[...].reshape(V * K, cols_b))
    cross = cross + split_dot(root_b, high_b[...], low_b[...], NT)
    for v in range(V):
        cross_out[v] = pack(cross[:, v * K : (v + 1) * K])
    cross_x[me] = cross_out[me]
    cross_copies = [
        send(cross_out.at[device["variant"]], cross_x.at[me], device) for device in to_x
    ]
    ends[me, :K, cols_a:] = root_b
    roots_b = gather_start(0, part_b)
    roots_c = gather_start(0, root_last)
    cross = total(cross_x, cross_copies)
    cross_copies = share(cross_y, y, cross, to_y)
    factor_relays = []
    for copy, origin in zip(factor_copies, (across, behind, ahead)):
        copy.wait_recv()
        factor_relays.append(send(factors.at[origin], factors.at[origin], {"variant": beside}))
    gather_relay(0, part_a, roots_a)
    cross = total(cross_y, cross_copies)
    cross_copies = share(cross_z, z, cross, to_z)
    gather_relay(0, part_b, roots_b)
    gather_relay(0, root_last, roots_c)
    for copy in factor_copies[3:] + factor_relays:
        copy.wait_recv()
    root_factor = unpack(factors[root])
    cross = unpack(total(cross_z, cross_copies))

    projection = dot(dot(root_factor, cross), factor, NT)
    eye = identity()
    rest = eye - MIDDLE * dot(projection, projection, NT)
    rest_2 = dot(rest, rest)
    rest_4 = dot(rest_2, rest_2)
    rest_8 = dot(rest_4, rest_4)
    inverse = eye + rest
    for rest in (rest_2, rest_4, rest_8):
        inverse = inverse + dot(inverse, rest)
    inverse = MIDDLE * inverse
    tangent_gram = inverse - eye
    turn = dot(inverse, dot(projection, factor))
    codes = [codes_ref[v] for v in range(V)]
    own_code = jnp.full((K, K), codes_ref[me], jnp.int32).astype(jnp.float32)
    weight = own_code / jnp.full((K, K), sum(codes[1:], codes[0]), jnp.int32).astype(jnp.float32)
    bend = weight * series(powers(tangent_gram), atan_coeffs)
    turn = dot(bend, turn)
    term_copies = share(terms, me, jnp.concatenate([turn, bend], axis=1), to_x)
    for copy in term_copies:
        copy.wait()
    bends = terms[0, :, K:]
    for v in range(1, V):
        bends = bends + terms[v, :, K:]
    back = dot(bends, root_factor)
    mixer = jnp.concatenate(
        [terms[v, :, :K] - jnp.where(root == v, back, 0.0) for v in range(V)], axis=1
    )
    part_a, part_b = pl.ds(0, cols_early), pl.ds(cols_early, cols_a - cols_early)
    part_c = pl.ds(cols_a, cols_b)
    blended_a = split_dot(mixer, high_a[:, :cols_early], low_a[:, :cols_early], NN)
    ends[me, K:, :cols_early] = blended_a
    blends_a = gather_start(K, part_a)
    blended_b = split_dot(mixer, high_a[:, cols_early:], low_a[:, cols_early:], NN)
    ends[me, K:, cols_early:cols_a] = blended_b
    blended_c = split_dot(mixer, high_b[...], low_b[...], NN)
    ends[me, K:, cols_a:] = blended_c
    energy = jnp.zeros((K, K), jnp.float32)
    for blended in (blended_a, blended_b, blended_c):
        energy = energy + split_dot(blended, *split(blended), NT)
    energy_copies = share(energy_x, me, pack(energy), to_x)
    blends_b = gather_start(K, part_b)
    blends_c = gather_start(K, part_c)
    root_groups = (roots_a, roots_b, roots_c)
    roots = [
        gather_beside(0, root_groups, (2,), behind, whole),
        gather_beside(0, root_groups, (3,), ahead, whole),
    ]
    energy = total(energy_x, energy_copies)
    energy_copies = share(energy_y, y, energy, to_y)
    gather_relay(K, part_a, blends_a)
    roots.append(gather_beside(0, root_groups, (5, 6), across, whole))
    energy = total(energy_y, energy_copies)
    energy_copies = share(energy_z, z, energy, to_z)
    gather_relay(K, part_b, blends_b)
    energy = unpack(total(energy_z, energy_copies))
    power = powers(energy)
    final = scale * jnp.concatenate(
        [dot(series(power, cos_coeffs), root_factor), series(power, sin_coeffs)], axis=1
    )

    gather_relay(K, part_c, blends_c)
    groups = (blends_a, blends_b, blends_c)
    blends = [
        gather_beside(K, groups, (2,), behind, whole), gather_beside(K, groups, (3,), ahead, whole)
    ]
    stores = []

    def finish(v, first, columns):
        part = pl.ds(first, columns)
        made[v, :, part] = split_dot(final, *split(ends[v, :, part]), NN)
        target = out_ref.at[:, pl.ds(pl.multiple_of(v * chunk + first, 128), columns)]
        store = pltpu.make_async_copy(made.at[v, :, part], target, local.at[3 + len(stores)])
        store.start()
        stores.append(store)

    for copy in [roots_a[4], roots_b[4], roots_c[4], *roots]:
        copy.wait_recv()
    finish(me, 0, chunk)
    finish(behind, 0, chunk)
    finish(ahead, 0, chunk)
    for copies in groups:
        copies[4].wait_recv()
    finish(beside, 0, chunk)
    early, late = pl.ds(0, cols_a), part_c
    for copy, dx in zip(blends, (3, 1)):
        copy.wait_recv()
        finish(variant(dx, 1), 0, chunk)
    blends.append(gather_beside(K, groups[:2], (5, 6), across, early))
    finish(across, 0, cols_a)
    blends.append(gather_beside(K, groups[2:], (5, 6), across, late))
    finish(across, cols_a, cols_b)
    blends[2].wait_recv()
    finish(variant(2, 1), 0, cols_a)
    blends[3].wait_recv()
    finish(variant(2, 1), cols_a, cols_b)
    gathers = roots_a + roots_b + roots_c + roots + blends_a + blends_b + blends_c + blends
    for copy in factor_copies + factor_relays + gathers:
        copy.wait_send()
    for store in stores:
        store.wait()


def on_device(size_z, size_y, snapshots, ref_index, weight_codes):
    snap = snapshots[0]
    rows = snap.shape[1]
    chunk = rows // V
    cols_a = max(256, chunk * 13 // 16 // 128 * 128)
    cols_b = chunk - cols_a
    cols_early = max(128, chunk // 8 // 128 * 128)
    sizes = (size_z, size_y, chunk, cols_a, cols_b, cols_early, math.sqrt(rows * size_z * size_y))
    small = (HALF, 2 * K)
    f32 = jnp.float32
    vmem = [
        (K, rows), (V, K, cols_a), (V, K, cols_b), (V, 2 * K, chunk), (V, K, chunk),
        (size_y, *small), (size_z, *small), (V, *small),
        (V, *small), (V, *small), (size_y, *small), (size_z, *small),
        (V, K, 2 * K), (V, *small), (size_y, *small), (size_z, *small),
    ]
    return pl.pallas_call(
        functools.partial(kernel, sizes),
        out_shape=jax.ShapeDtypeStruct((K, rows), f32),
        in_specs=[
            pl.BlockSpec(memory_space=pltpu.SMEM),
            pl.BlockSpec(memory_space=pltpu.SMEM),
            pl.BlockSpec(memory_space=pltpu.HBM),
        ],
        out_specs=pl.BlockSpec(memory_space=pl.ANY),
        scratch_shapes=[pltpu.VMEM(shape, f32) for shape in vmem]
        + [pltpu.VMEM((V * K, cols), jnp.bfloat16) for cols in (cols_a, cols_a, cols_b, cols_b)]
        + [
            pltpu.SemaphoreType.DMA((160,)),
            pltpu.SemaphoreType.DMA((160,)),
            pltpu.SemaphoreType.DMA((16,)),
        ],
        compiler_params=pltpu.CompilerParams(
            collective_id=0, has_side_effects=True, vmem_limit_bytes=40 << 20
        ),
        name="interpolate",
    )(ref_index, pltpu.with_memory_space_constraint(weight_codes, pltpu.HBM), pltpu.with_memory_space_constraint(snap, pltpu.HBM))


def solution(mesh, size_y=4):
    size_z = mesh.shape["mesh"] // size_y
    placed = (P("variant", None, "mesh"), P(), P())
    return jax.shard_map(
        functools.partial(on_device, size_z, size_y),
        mesh=mesh, in_specs=placed, out_specs=P(None, "mesh"), check_vma=False,
    )
```

```python
import functools
import math

import jax
import jax.numpy as jnp
from jax import lax
from jax.experimental import pallas as pl
from jax.experimental.pallas import tpu as pltpu
from jax.sharding import PartitionSpec as P

MESH = pl.DeviceIdType.MESH
HIGHEST = lax.Precision.HIGHEST
K = 64
V = 8
HALF = K // 2
atan_coeffs = [(-1.0) ** k / (2 * k + 1) for k in range(24)]
cos_coeffs = [(-1.0) ** k / math.factorial(2 * k) for k in range(24)]
sin_coeffs = [(-1.0) ** k / math.factorial(2 * k + 1) for k in range(24)]
MIDDLE = 2.0 / (1.0 + 1.0 / 1.64)


def dot(left, right, contract=((1,), (0,))):
    return lax.dot_general(
        left, right, (contract, ((), ())), precision=HIGHEST, preferred_element_type=jnp.float32
    )


NT = ((1,), (1,))
NN = ((1,), (0,))


def split(array):
    high = array.astype(jnp.bfloat16)
    return high, (array - high.astype(jnp.float32)).astype(jnp.bfloat16)


def split_dot(left, high, low, contract):
    rows = left.shape[0]
    left_high, left_low = split(left)
    both = lax.dot_general(
        jnp.concatenate([left_high, left_low], axis=0), high, (contract, ((), ())),
        preferred_element_type=jnp.float32,
    )
    other = lax.dot_general(
        left_high, low, (contract, ((), ())), preferred_element_type=jnp.float32
    )
    return both[:rows] + (both[rows:] + other)


def identity():
    rows = lax.broadcasted_iota(jnp.int32, (K, K), 0)
    columns = lax.broadcasted_iota(jnp.int32, (K, K), 1)
    return jnp.where(rows == columns, 1.0, 0.0).astype(jnp.float32)


def pack(square):
    return jnp.concatenate([square[:HALF], square[HALF:]], axis=1)


def unpack(packed):
    return jnp.concatenate([packed[:, :K], packed[:, K:]], axis=0)


def powers(matrix):
    second = dot(matrix, matrix)
    third = dot(second, matrix)
    fourth = dot(second, second)
    return [
        identity(), matrix, second, third, fourth,
        dot(fourth, matrix), dot(fourth, second), dot(fourth, third), dot(fourth, fourth),
    ]


def group(power, coeffs):
    total = coeffs[0] * power[0]
    for i in range(1, len(coeffs)):
        total = total + coeffs[i] * power[i]
    return total


def series(power, coeffs):
    high = group(power, coeffs[16:24])
    middle = group(power, coeffs[8:16]) + dot(power[8], high)
    return group(power, coeffs[0:8]) + dot(power[8], middle)


def inverse_factor(gram):
    rows = lax.broadcasted_iota(jnp.int32, (K, 2 * K), 0)
    columns = lax.broadcasted_iota(jnp.int32, (K, 2 * K), 1)
    top = lax.broadcasted_iota(jnp.int32, (1, 2 * K), 1)

    def step(j, both):
        row = jnp.sum(jnp.where(rows == j, both, 0.0), axis=0, keepdims=True)
        column = jnp.sum(jnp.where(columns == j, both, 0.0), axis=1, keepdims=True)
        pivot = jnp.sum(jnp.where(top == j, row, 0.0), axis=1, keepdims=True)
        return both - jnp.where(rows > j, column, 0.0) * (row / pivot)

    both = lax.fori_loop(0, K, step, jnp.concatenate([gram, identity()], axis=1))
    pivots = jnp.sum(jnp.where(rows == columns, both, 0.0), axis=1, keepdims=True)
    return both[:, K:] * (1.0 / jnp.sqrt(pivots))


def kernel(
    sizes, root_ref, codes_ref, snap_ref, out_ref,
    own, stack_a, stack_b, ends, made,
    gram_y, gram_z, factors, cross_out, cross_x, cross_y, cross_z, terms, energy_x, energy_y, energy_z,
    high_a, low_a, high_b, low_b, sent, got, local,
):
    size_z, size_y, chunk, cols_a, cols_b, cols_early, scale = sizes
    me = lax.axis_index("variant")
    place = lax.axis_index("mesh")
    chip, core = me // 2, lax.rem(me, 2)
    z, y = place // size_y, lax.rem(place, size_y)
    count = iter(range(1000))

    def variant(dx, dc):
        return lax.rem(chip + dx, 4) * 2 + lax.rem(core + dc, 2)

    x_order = [(2, 0), (2, 1), (1, 0), (3, 0), (1, 1), (3, 1), (0, 1)]
    to_x = [{"variant": variant(dx, dc)} for dx, dc in x_order]
    to_y = [{"mesh": z * size_y + lax.rem(y + d, size_y)} for d in range(1, size_y)]
    to_z = [{"mesh": lax.rem(z + d, size_z) * size_y + y} for d in range(1, size_z)]

    def send(source, target, device):
        i = next(count)
        copy = pltpu.make_async_remote_copy(
            src_ref=source, dst_ref=target, send_sem=sent.at[i], recv_sem=got.at[i],
            device_id=device, device_id_type=MESH,
        )
        copy.start()
        return copy

    def share(buffer, slot, value, devices):
        buffer[slot] = value
        return [send(buffer.at[slot], buffer.at[slot], device) for device in devices]

    def total(buffer, copies):
        for copy in copies:
            copy.wait()
        result = buffer[0]
        for i in range(1, buffer.shape[0]):
            result = result + buffer[i]
        return result

    own_copy = pltpu.make_async_copy(snap_ref, own, local.at[0])
    own_copy.start()
    mine = pl.multiple_of(me * chunk, chunk)
    keep_a = pltpu.make_async_copy(
        snap_ref.at[:, pl.ds(mine, cols_a)], stack_a.at[me], local.at[1]
    )
    keep_b = pltpu.make_async_copy(
        snap_ref.at[:, pl.ds(pl.multiple_of(mine + cols_a, 128), cols_b)], stack_b.at[me], local.at[2]
    )
    keep_a.start()
    keep_b.start()

    barrier = pltpu.get_barrier_semaphore()
    for device in to_x + to_y + to_z:
        pl.semaphore_signal(barrier, inc=1, device_id=device, device_id_type=MESH)
    pl.semaphore_wait(barrier, len(to_x) + len(to_y) + len(to_z))

    stage_a = []
    for device in to_x:
        first = pl.multiple_of(device["variant"] * chunk, chunk)
        stage_a.append(send(snap_ref.at[:, pl.ds(first, cols_a)], stack_a.at[me], device))

    stage_b = []
    for device in to_x:
        first = pl.multiple_of(device["variant"] * chunk + cols_a, 128)
        stage_b.append(send(snap_ref.at[:, pl.ds(first, cols_b)], stack_b.at[me], device))

    own_copy.wait()

    def gram_step(i, gram):
        block = own[:, pl.ds(pl.multiple_of(i * chunk, chunk), chunk)]
        return gram + dot(block, block, NT)

    gram = lax.fori_loop(0, V, gram_step, jnp.zeros((K, K), jnp.float32))
    gram = total(gram_y, share(gram_y, y, pack(gram), to_y))
    gram = total(gram_z, share(gram_z, z, gram, to_z))
    factor = inverse_factor(unpack(gram))
    ahead, behind, beside, across = variant(1, 0), variant(3, 0), variant(0, 1), variant(2, 0)
    factor_copies = share(
        factors, me, pack(factor), [{"variant": v} for v in (across, ahead, behind, beside)]
    )

    def gather_start(row, columns):
        upper, lower, both = pl.ds(row, HALF), pl.ds(row + HALF, HALF), pl.ds(row, K)
        copies = []
        for rows, device in [(upper, ahead), (lower, behind), (lower, ahead), (upper, behind), (both, beside)]:
            part = ends.at[me, rows, columns]
            copies.append(send(part, part, {"variant": device}))
        return copies

    def gather_relay(row, columns, copies):
        for first, rows, origin, device in [
            (copies[0], pl.ds(row, HALF), behind, ahead),
            (copies[1], pl.ds(row + HALF, HALF), ahead, behind),
        ]:
            first.wait_recv()
            part = ends.at[origin, rows, columns]
            copies.append(send(part, part, {"variant": device}))

    def gather_beside(row, groups, needs, origin, columns):
        for copies in groups:
            for i in needs:
                copies[i].wait_recv()
        part = ends.at[origin, pl.ds(row, K), columns]
        return send(part, part, {"variant": beside})

    whole = pl.ds(0, chunk)
    part_a, part_b = pl.ds(0, chunk // 4), pl.ds(chunk // 4, chunk // 2)
    root_last = pl.ds(chunk - chunk // 4, chunk // 4)

    keep_a.wait()
    keep_b.wait()
    for copy in stage_a:
        copy.wait()
    root = root_ref[0]
    root_a = stack_a[root]
    ends[me, :K, :cols_a] = root_a
    roots_a = gather_start(0, part_a)
    high_a[...], low_a[...] = split(stack_a[...].reshape(V * K, cols_a))
    cross = split_dot(root_a, high_a[...], low_a[...], NT)
    for copy in stage_b:
        copy.wait()
    root_b = stack_b[root]
    high_b[...], low_b[...] = split(stack_b[...].reshape(V * K, cols_b))
    cross = cross + split_dot(root_b, high_b[...], low_b[...], NT)
    for v in range(V):
        cross_out[v] = pack(cross[:, v * K : (v + 1) * K])
    cross_x[me] = cross_out[me]
    cross_copies = [
        send(cross_out.at[device["variant"]], cross_x.at[me], device) for device in to_x
    ]
    ends[me, :K, cols_a:] = root_b
    roots_b = gather_start(0, part_b)
    roots_c = gather_start(0, root_last)
    cross = total(cross_x, cross_copies)
    cross_copies = share(cross_y, y, cross, to_y)
    factor_relays = []
    for copy, origin in zip(factor_copies, (across, behind, ahead)):
        copy.wait_recv()
        factor_relays.append(send(factors.at[origin], factors.at[origin], {"variant": beside}))
    gather_relay(0, part_a, roots_a)
    cross = total(cross_y, cross_copies)
    cross_copies = share(cross_z, z, cross, to_z)
    gather_relay(0, part_b, roots_b)
    gather_relay(0, root_last, roots_c)
    for copy in factor_copies[3:] + factor_relays:
        copy.wait_recv()
    root_factor = unpack(factors[root])
    cross = unpack(total(cross_z, cross_copies))

    projection = dot(dot(root_factor, cross), factor, NT)
    eye = identity()
    rest = eye - MIDDLE * dot(projection, projection, NT)
    rest_2 = dot(rest, rest)
    rest_4 = dot(rest_2, rest_2)
    rest_8 = dot(rest_4, rest_4)
    inverse = eye + rest
    for rest in (rest_2, rest_4, rest_8):
        inverse = inverse + dot(inverse, rest)
    inverse = MIDDLE * inverse
    tangent_gram = inverse - eye
    turn = dot(inverse, dot(projection, factor))
    codes = [codes_ref[v] for v in range(V)]
    own_code = jnp.full((K, K), codes_ref[me], jnp.int32).astype(jnp.float32)
    weight = own_code / jnp.full((K, K), sum(codes[1:], codes[0]), jnp.int32).astype(jnp.float32)
    bend = weight * series(powers(tangent_gram), atan_coeffs)
    turn = dot(bend, turn)
    term_copies = share(terms, me, jnp.concatenate([turn, bend], axis=1), to_x)
    for copy in term_copies:
        copy.wait()
    bends = terms[0, :, K:]
    for v in range(1, V):
        bends = bends + terms[v, :, K:]
    back = dot(bends, root_factor)
    mixer = jnp.concatenate(
        [terms[v, :, :K] - jnp.where(root == v, back, 0.0) for v in range(V)], axis=1
    )
    part_a, part_b = pl.ds(0, cols_early), pl.ds(cols_early, cols_a - cols_early)
    part_c = pl.ds(cols_a, cols_b)
    blended_a = split_dot(mixer, high_a[:, :cols_early], low_a[:, :cols_early], NN)
    ends[me, K:, :cols_early] = blended_a
    blends_a = gather_start(K, part_a)
    blended_b = split_dot(mixer, high_a[:, cols_early:], low_a[:, cols_early:], NN)
    ends[me, K:, cols_early:cols_a] = blended_b
    blended_c = split_dot(mixer, high_b[...], low_b[...], NN)
    ends[me, K:, cols_a:] = blended_c
    energy = jnp.zeros((K, K), jnp.float32)
    for blended in (blended_a, blended_b, blended_c):
        energy = energy + split_dot(blended, *split(blended), NT)
    energy_copies = share(
        energy_x, me, pack(energy), [{"variant": v} for v in (across, ahead, behind, beside)]
    )
    blends_b = gather_start(K, part_b)
    blends_c = gather_start(K, part_c)
    root_groups = (roots_a, roots_b, roots_c)
    roots = [
        gather_beside(0, root_groups, (2,), behind, whole),
        gather_beside(0, root_groups, (3,), ahead, whole),
    ]
    for copy, origin in zip(energy_copies[:3], (across, behind, ahead)):
        copy.wait_recv()
        energy_copies.append(send(energy_x.at[origin], energy_x.at[origin], {"variant": beside}))
    for copy in energy_copies[:3]:
        copy.wait_send()
    energy = total(energy_x, energy_copies[3:])
    energy_copies = share(energy_y, y, energy, to_y)
    gather_relay(K, part_a, blends_a)
    roots.append(gather_beside(0, root_groups, (5, 6), across, whole))
    energy = total(energy_y, energy_copies)
    energy_copies = share(energy_z, z, energy, to_z)
    gather_relay(K, part_b, blends_b)
    energy = unpack(total(energy_z, energy_copies))
    power = powers(energy)
    final = scale * jnp.concatenate(
        [dot(series(power, cos_coeffs), root_factor), series(power, sin_coeffs)], axis=1
    )

    gather_relay(K, part_c, blends_c)
    groups = (blends_a, blends_b, blends_c)
    blends = [
        gather_beside(K, groups, (2,), behind, whole), gather_beside(K, groups, (3,), ahead, whole)
    ]
    stores = []

    def finish(v, first, columns):
        part = pl.ds(first, columns)
        made[v, :, part] = split_dot(final, *split(ends[v, :, part]), NN)
        target = out_ref.at[:, pl.ds(pl.multiple_of(v * chunk + first, 128), columns)]
        store = pltpu.make_async_copy(made.at[v, :, part], target, local.at[3 + len(stores)])
        store.start()
        stores.append(store)

    for copy in [roots_a[4], roots_b[4], roots_c[4], *roots]:
        copy.wait_recv()
    finish(me, 0, chunk)
    finish(behind, 0, chunk)
    finish(ahead, 0, chunk)
    for copies in groups:
        copies[4].wait_recv()
    finish(beside, 0, chunk)
    early, late = pl.ds(0, cols_a), part_c
    for copy, dx in zip(blends, (3, 1)):
        copy.wait_recv()
        finish(variant(dx, 1), 0, chunk)
    blends.append(gather_beside(K, groups[:2], (5, 6), across, early))
    finish(across, 0, cols_a)
    blends.append(gather_beside(K, groups[2:], (5, 6), across, late))
    finish(across, cols_a, cols_b)
    blends[2].wait_recv()
    finish(variant(2, 1), 0, cols_a)
    blends[3].wait_recv()
    finish(variant(2, 1), cols_a, cols_b)
    gathers = roots_a + roots_b + roots_c + roots + blends_a + blends_b + blends_c + blends
    for copy in factor_copies + factor_relays + gathers:
        copy.wait_send()
    for store in stores:
        store.wait()


def on_device(size_z, size_y, snapshots, ref_index, weight_codes):
    snap = snapshots[0]
    rows = snap.shape[1]
    chunk = rows // V
    cols_a = max(256, chunk * 13 // 16 // 128 * 128)
    cols_b = chunk - cols_a
    cols_early = max(128, chunk // 8 // 128 * 128)
    sizes = (size_z, size_y, chunk, cols_a, cols_b, cols_early, math.sqrt(rows * size_z * size_y))
    small = (HALF, 2 * K)
    f32 = jnp.float32
    vmem = [
        (K, rows), (V, K, cols_a), (V, K, cols_b), (V, 2 * K, chunk), (V, K, chunk),
        (size_y, *small), (size_z, *small), (V, *small),
        (V, *small), (V, *small), (size_y, *small), (size_z, *small),
        (V, K, 2 * K), (V, *small), (size_y, *small), (size_z, *small),
    ]
    return pl.pallas_call(
        functools.partial(kernel, sizes),
        out_shape=jax.ShapeDtypeStruct((K, rows), f32),
        in_specs=[
            pl.BlockSpec(memory_space=pltpu.SMEM),
            pl.BlockSpec(memory_space=pltpu.SMEM),
            pl.BlockSpec(memory_space=pltpu.HBM),
        ],
        out_specs=pl.BlockSpec(memory_space=pl.ANY),
        scratch_shapes=[pltpu.VMEM(shape, f32) for shape in vmem]
        + [pltpu.VMEM((V * K, cols), jnp.bfloat16) for cols in (cols_a, cols_a, cols_b, cols_b)]
        + [
            pltpu.SemaphoreType.DMA((160,)),
            pltpu.SemaphoreType.DMA((160,)),
            pltpu.SemaphoreType.DMA((16,)),
        ],
        compiler_params=pltpu.CompilerParams(
            collective_id=0, has_side_effects=True, vmem_limit_bytes=40 << 20
        ),
        name="interpolate",
    )(ref_index, pltpu.with_memory_space_constraint(weight_codes, pltpu.HBM), pltpu.with_memory_space_constraint(snap, pltpu.HBM))


def solution(mesh, size_y=4):
    size_z = mesh.shape["mesh"] // size_y
    placed = (P("variant", None, "mesh"), P(), P())
    return jax.shard_map(
        functools.partial(on_device, size_z, size_y),
        mesh=mesh, in_specs=placed, out_specs=P(None, "mesh"), check_vma=False,
    )
```

```python
import functools
import math

import jax
import jax.numpy as jnp
from jax import lax
from jax.experimental import pallas as pl
from jax.experimental.pallas import tpu as pltpu
from jax.sharding import PartitionSpec as P

MESH = pl.DeviceIdType.MESH
HIGHEST = lax.Precision.HIGHEST
K = 64
V = 8
HALF = K // 2
atan_coeffs = [(-1.0) ** k / (2 * k + 1) for k in range(24)]
cos_coeffs = [(-1.0) ** k / math.factorial(2 * k) for k in range(24)]
sin_coeffs = [(-1.0) ** k / math.factorial(2 * k + 1) for k in range(24)]
MIDDLE = 2.0 / (1.0 + 1.0 / 1.64)


def dot(left, right, contract=((1,), (0,))):
    return lax.dot_general(
        left, right, (contract, ((), ())), precision=HIGHEST, preferred_element_type=jnp.float32
    )


NT = ((1,), (1,))
NN = ((1,), (0,))


def split(array):
    high = array.astype(jnp.bfloat16)
    return high, (array - high.astype(jnp.float32)).astype(jnp.bfloat16)


def split_dot(left, high, low, contract):
    rows = left.shape[0]
    left_high, left_low = split(left)
    both = lax.dot_general(
        jnp.concatenate([left_high, left_low], axis=0), high, (contract, ((), ())),
        preferred_element_type=jnp.float32,
    )
    other = lax.dot_general(
        left_high, low, (contract, ((), ())), preferred_element_type=jnp.float32
    )
    return both[:rows] + (both[rows:] + other)


def identity():
    rows = lax.broadcasted_iota(jnp.int32, (K, K), 0)
    columns = lax.broadcasted_iota(jnp.int32, (K, K), 1)
    return jnp.where(rows == columns, 1.0, 0.0).astype(jnp.float32)


def pack(square):
    return jnp.concatenate([square[:HALF], square[HALF:]], axis=1)


def unpack(packed):
    return jnp.concatenate([packed[:, :K], packed[:, K:]], axis=0)


def powers(matrix):
    second = dot(matrix, matrix)
    third = dot(second, matrix)
    fourth = dot(second, second)
    return [
        identity(), matrix, second, third, fourth,
        dot(fourth, matrix), dot(fourth, second), dot(fourth, third), dot(fourth, fourth),
    ]


def group(power, coeffs):
    total = coeffs[0] * power[0]
    for i in range(1, len(coeffs)):
        total = total + coeffs[i] * power[i]
    return total


def series(power, coeffs):
    high = group(power, coeffs[16:24])
    middle = group(power, coeffs[8:16]) + dot(power[8], high)
    return group(power, coeffs[0:8]) + dot(power[8], middle)


def inverse_factor(gram):
    rows = lax.broadcasted_iota(jnp.int32, (K, 2 * K), 0)
    columns = lax.broadcasted_iota(jnp.int32, (K, 2 * K), 1)
    top = lax.broadcasted_iota(jnp.int32, (1, 2 * K), 1)

    def step(j, both):
        row = jnp.sum(jnp.where(rows == j, both, 0.0), axis=0, keepdims=True)
        column = jnp.sum(jnp.where(columns == j, both, 0.0), axis=1, keepdims=True)
        pivot = jnp.sum(jnp.where(top == j, row, 0.0), axis=1, keepdims=True)
        return both - jnp.where(rows > j, column, 0.0) * (row / pivot)

    both = lax.fori_loop(0, K, step, jnp.concatenate([gram, identity()], axis=1))
    pivots = jnp.sum(jnp.where(rows == columns, both, 0.0), axis=1, keepdims=True)
    return both[:, K:] * (1.0 / jnp.sqrt(pivots))


def kernel(
    sizes, root_ref, codes_ref, snap_ref, out_ref,
    own, stack_a, stack_b, ends, made,
    gram_y, gram_z, factors, cross_out, cross_x, cross_y, cross_z, terms, energy_x, energy_y, energy_z,
    high_a, low_a, high_b, low_b, sent, got, local,
):
    size_z, size_y, chunk, cols_a, cols_b, cols_early, scale = sizes
    me = lax.axis_index("variant")
    place = lax.axis_index("mesh")
    chip, core = me // 2, lax.rem(me, 2)
    z, y = place // size_y, lax.rem(place, size_y)
    count = iter(range(1000))

    def variant(dx, dc):
        return lax.rem(chip + dx, 4) * 2 + lax.rem(core + dc, 2)

    x_order = [(2, 0), (2, 1), (1, 0), (3, 0), (1, 1), (3, 1), (0, 1)]
    to_x = [{"variant": variant(dx, dc)} for dx, dc in x_order]
    to_y = [{"mesh": z * size_y + lax.rem(y + d, size_y)} for d in range(1, size_y)]
    to_z = [{"mesh": lax.rem(z + d, size_z) * size_y + y} for d in range(1, size_z)]

    def send(source, target, device):
        i = next(count)
        copy = pltpu.make_async_remote_copy(
            src_ref=source, dst_ref=target, send_sem=sent.at[i], recv_sem=got.at[i],
            device_id=device, device_id_type=MESH,
        )
        copy.start()
        return copy

    def share(buffer, slot, value, devices):
        buffer[slot] = value
        return [send(buffer.at[slot], buffer.at[slot], device) for device in devices]

    def total(buffer, copies):
        for copy in copies:
            copy.wait()
        result = buffer[0]
        for i in range(1, buffer.shape[0]):
            result = result + buffer[i]
        return result

    own_copy = pltpu.make_async_copy(snap_ref, own, local.at[0])
    own_copy.start()
    mine = pl.multiple_of(me * chunk, chunk)
    keep_a = pltpu.make_async_copy(
        snap_ref.at[:, pl.ds(mine, cols_a)], stack_a.at[me], local.at[1]
    )
    keep_b = pltpu.make_async_copy(
        snap_ref.at[:, pl.ds(pl.multiple_of(mine + cols_a, 128), cols_b)], stack_b.at[me], local.at[2]
    )
    keep_a.start()
    keep_b.start()

    barrier = pltpu.get_barrier_semaphore()
    for device in to_x + to_y + to_z:
        pl.semaphore_signal(barrier, inc=1, device_id=device, device_id_type=MESH)
    pl.semaphore_wait(barrier, len(to_x) + len(to_y) + len(to_z))

    stage_a = []
    for device in to_x:
        first = pl.multiple_of(device["variant"] * chunk, chunk)
        stage_a.append(send(snap_ref.at[:, pl.ds(first, cols_a)], stack_a.at[me], device))

    stage_b = []
    for device in to_x:
        first = pl.multiple_of(device["variant"] * chunk + cols_a, 128)
        stage_b.append(send(snap_ref.at[:, pl.ds(first, cols_b)], stack_b.at[me], device))

    own_copy.wait()

    def gram_step(i, gram):
        block = own[:, pl.ds(pl.multiple_of(i * chunk, chunk), chunk)]
        return gram + dot(block, block, NT)

    gram = lax.fori_loop(0, V, gram_step, jnp.zeros((K, K), jnp.float32))
    gram = total(gram_y, share(gram_y, y, pack(gram), to_y))
    gram = total(gram_z, share(gram_z, z, gram, to_z))
    factor = inverse_factor(unpack(gram))
    ahead, behind, beside, across = variant(1, 0), variant(3, 0), variant(0, 1), variant(2, 0)
    factor_copies = share(
        factors, me, pack(factor), [{"variant": v} for v in (across, ahead, behind, beside)]
    )

    def gather_start(row, columns):
        upper, lower, both = pl.ds(row, HALF), pl.ds(row + HALF, HALF), pl.ds(row, K)
        copies = []
        for rows, device in [(upper, ahead), (lower, behind), (lower, ahead), (upper, behind), (both, beside)]:
            part = ends.at[me, rows, columns]
            copies.append(send(part, part, {"variant": device}))
        return copies

    def gather_relay(row, columns, copies):
        for first, rows, origin, device in [
            (copies[0], pl.ds(row, HALF), behind, ahead),
            (copies[1], pl.ds(row + HALF, HALF), ahead, behind),
        ]:
            first.wait_recv()
            part = ends.at[origin, rows, columns]
            copies.append(send(part, part, {"variant": device}))

    def gather_beside(row, groups, needs, origin, columns):
        for copies in groups:
            for i in needs:
                copies[i].wait_recv()
        part = ends.at[origin, pl.ds(row, K), columns]
        return send(part, part, {"variant": beside})

    whole = pl.ds(0, chunk)
    part_a, part_b = pl.ds(0, chunk // 4), pl.ds(chunk // 4, chunk // 2)
    root_last = pl.ds(chunk - chunk // 4, chunk // 4)

    keep_a.wait()
    keep_b.wait()
    for copy in stage_a:
        copy.wait()
    root = root_ref[0]
    root_a = stack_a[root]
    ends[me, :K, :cols_a] = root_a
    roots_a = gather_start(0, part_a)
    high_a[...], low_a[...] = split(stack_a[...].reshape(V * K, cols_a))
    cross = split_dot(root_a, high_a[...], low_a[...], NT)
    for copy in stage_b:
        copy.wait()
    root_b = stack_b[root]
    high_b[...], low_b[...] = split(stack_b[...].reshape(V * K, cols_b))
    cross = cross + split_dot(root_b, high_b[...], low_b[...], NT)
    for v in range(V):
        cross_out[v] = pack(cross[:, v * K : (v + 1) * K])
    cross_x[me] = cross_out[me]
    cross_copies = [
        send(cross_out.at[device["variant"]], cross_x.at[me], device) for device in to_x
    ]
    ends[me, :K, cols_a:] = root_b
    roots_b = gather_start(0, part_b)
    roots_c = gather_start(0, root_last)
    cross = total(cross_x, cross_copies)
    cross_copies = share(cross_y, y, cross, to_y)
    factor_relays = []
    for copy, origin in zip(factor_copies, (across, behind, ahead)):
        copy.wait_recv()
        factor_relays.append(send(factors.at[origin], factors.at[origin], {"variant": beside}))
    gather_relay(0, part_a, roots_a)
    cross = total(cross_y, cross_copies)
    cross_copies = share(cross_z, z, cross, to_z)
    gather_relay(0, part_b, roots_b)
    gather_relay(0, root_last, roots_c)
    for copy in factor_copies[3:] + factor_relays:
        copy.wait_recv()
    root_factor = unpack(factors[root])
    cross = unpack(total(cross_z, cross_copies))

    projection = dot(dot(root_factor, cross), factor, NT)
    eye = identity()
    rest = eye - MIDDLE * dot(projection, projection, NT)
    rest_2 = dot(rest, rest)
    rest_4 = dot(rest_2, rest_2)
    rest_8 = dot(rest_4, rest_4)
    inverse = eye + rest
    for rest in (rest_2, rest_4, rest_8):
        inverse = inverse + dot(inverse, rest)
    inverse = MIDDLE * inverse
    tangent_gram = inverse - eye
    turn = dot(inverse, dot(projection, factor))
    codes = [codes_ref[v] for v in range(V)]
    own_code = jnp.full((K, K), codes_ref[me], jnp.int32).astype(jnp.float32)
    weight = own_code / jnp.full((K, K), sum(codes[1:], codes[0]), jnp.int32).astype(jnp.float32)
    bend = weight * series(powers(tangent_gram), atan_coeffs)
    turn = dot(bend, turn)
    term_copies = share(terms, me, jnp.concatenate([turn, bend], axis=1), to_x)
    for copy in term_copies:
        copy.wait()
    bends = terms[0, :, K:]
    for v in range(1, V):
        bends = bends + terms[v, :, K:]
    back = dot(bends, root_factor)
    mixer = jnp.concatenate(
        [terms[v, :, :K] - jnp.where(root == v, back, 0.0) for v in range(V)], axis=1
    )
    part_a, part_b = pl.ds(0, cols_early), pl.ds(cols_early, cols_a - cols_early)
    part_c = pl.ds(cols_a, cols_b)
    blended_a = split_dot(mixer, high_a[:, :cols_early], low_a[:, :cols_early], NN)
    ends[me, K:, :cols_early] = blended_a
    blends_a = gather_start(K, part_a)
    blended_b = split_dot(mixer, high_a[:, cols_early:], low_a[:, cols_early:], NN)
    ends[me, K:, cols_early:cols_a] = blended_b
    blended_c = split_dot(mixer, high_b[...], low_b[...], NN)
    ends[me, K:, cols_a:] = blended_c
    energy = jnp.zeros((K, K), jnp.float32)
    for blended in (blended_a, blended_b, blended_c):
        energy = energy + split_dot(blended, *split(blended), NT)
    energy_copies = share(
        energy_x, me, pack(energy), [{"variant": v} for v in (across, ahead, behind, beside)]
    )
    blends_b = gather_start(K, part_b)
    blends_c = gather_start(K, part_c)
    root_groups = (roots_a, roots_b, roots_c)
    roots = [
        gather_beside(0, root_groups, (2,), behind, whole),
        gather_beside(0, root_groups, (3,), ahead, whole),
    ]
    for copy, origin in zip(energy_copies[:3], (across, behind, ahead)):
        copy.wait_recv()
        energy_copies.append(send(energy_x.at[origin], energy_x.at[origin], {"variant": beside}))
    for copy in energy_copies[:3]:
        copy.wait_send()
    energy = total(energy_x, energy_copies[3:])
    energy_copies = share(energy_y, y, energy, to_y)
    gather_relay(K, part_a, blends_a)
    roots.append(gather_beside(0, root_groups, (5, 6), across, whole))
    energy = total(energy_y, energy_copies)
    energy_copies = share(energy_z, z, energy, to_z)
    gather_relay(K, part_b, blends_b)
    gather_relay(K, part_c, blends_c)
    energy = unpack(total(energy_z, energy_copies))
    power = powers(energy)
    final = scale * jnp.concatenate(
        [dot(series(power, cos_coeffs), root_factor), series(power, sin_coeffs)], axis=1
    )

    groups = (blends_a, blends_b, blends_c)
    blends = [
        gather_beside(K, groups, (2,), behind, whole), gather_beside(K, groups, (3,), ahead, whole)
    ]
    stores = []

    def finish(v, first, columns):
        part = pl.ds(first, columns)
        made[v, :, part] = split_dot(final, *split(ends[v, :, part]), NN)
        target = out_ref.at[:, pl.ds(pl.multiple_of(v * chunk + first, 128), columns)]
        store = pltpu.make_async_copy(made.at[v, :, part], target, local.at[3 + len(stores)])
        store.start()
        stores.append(store)

    for copy in [roots_a[4], roots_b[4], roots_c[4], *roots]:
        copy.wait_recv()
    finish(me, 0, chunk)
    finish(behind, 0, chunk)
    finish(ahead, 0, chunk)
    for copies in groups:
        copies[4].wait_recv()
    finish(beside, 0, chunk)
    early, late = pl.ds(0, cols_a), part_c
    for copy, dx in zip(blends, (3, 1)):
        copy.wait_recv()
        finish(variant(dx, 1), 0, chunk)
    blends.append(gather_beside(K, groups[:2], (5, 6), across, early))
    finish(across, 0, cols_a)
    blends.append(gather_beside(K, groups[2:], (5, 6), across, late))
    finish(across, cols_a, cols_b)
    blends[2].wait_recv()
    finish(variant(2, 1), 0, cols_a)
    blends[3].wait_recv()
    finish(variant(2, 1), cols_a, cols_b)
    gathers = roots_a + roots_b + roots_c + roots + blends_a + blends_b + blends_c + blends
    for copy in factor_copies + factor_relays + gathers:
        copy.wait_send()
    for store in stores:
        store.wait()


def on_device(size_z, size_y, snapshots, ref_index, weight_codes):
    snap = snapshots[0]
    rows = snap.shape[1]
    chunk = rows // V
    cols_a = max(256, chunk * 13 // 16 // 128 * 128)
    cols_b = chunk - cols_a
    cols_early = max(128, chunk // 8 // 128 * 128)
    sizes = (size_z, size_y, chunk, cols_a, cols_b, cols_early, math.sqrt(rows * size_z * size_y))
    small = (HALF, 2 * K)
    f32 = jnp.float32
    vmem = [
        (K, rows), (V, K, cols_a), (V, K, cols_b), (V, 2 * K, chunk), (V, K, chunk),
        (size_y, *small), (size_z, *small), (V, *small),
        (V, *small), (V, *small), (size_y, *small), (size_z, *small),
        (V, K, 2 * K), (V, *small), (size_y, *small), (size_z, *small),
    ]
    return pl.pallas_call(
        functools.partial(kernel, sizes),
        out_shape=jax.ShapeDtypeStruct((K, rows), f32),
        in_specs=[
            pl.BlockSpec(memory_space=pltpu.SMEM),
            pl.BlockSpec(memory_space=pltpu.SMEM),
            pl.BlockSpec(memory_space=pltpu.HBM),
        ],
        out_specs=pl.BlockSpec(memory_space=pl.ANY),
        scratch_shapes=[pltpu.VMEM(shape, f32) for shape in vmem]
        + [pltpu.VMEM((V * K, cols), jnp.bfloat16) for cols in (cols_a, cols_a, cols_b, cols_b)]
        + [
            pltpu.SemaphoreType.DMA((160,)),
            pltpu.SemaphoreType.DMA((160,)),
            pltpu.SemaphoreType.DMA((16,)),
        ],
        compiler_params=pltpu.CompilerParams(
            collective_id=0, has_side_effects=True, vmem_limit_bytes=40 << 20
        ),
        name="interpolate",
    )(ref_index, pltpu.with_memory_space_constraint(weight_codes, pltpu.HBM), pltpu.with_memory_space_constraint(snap, pltpu.HBM))


def solution(mesh, size_y=4):
    size_z = mesh.shape["mesh"] // size_y
    placed = (P("variant", None, "mesh"), P(), P())
    return jax.shard_map(
        functools.partial(on_device, size_z, size_y),
        mesh=mesh, in_specs=placed, out_specs=P(None, "mesh"), check_vma=False,
    )
```
